256 devices in a mesh: store: 64 (over z, x, core), batch: 4 (over y).
Axes of the slice: x: 4, y: 4, z: 8, core: 2. Of those that a mesh axis runs over, the one named last changes fastest.
Arguments:
- queries: bfloat16 [32768, 1152], P(('store', 'batch')), may hold values from -6 to 6
- query_cluster: int32 [32768], P(('store', 'batch')), may hold values from 0 to 63, as said below
- store: bfloat16 [131072, 1152], P('store'), may hold values from -6 to 6
- store_counts: int32 [64], replicated, may hold values from 2 to 2048, as said below
Outputs:
- best_two: float32 [32768, 2], P(('store', 'batch'))
- novelty: float32 [32768], P(('store', 'batch'))
- neighbours: float32 [32768, 1152], P(('store', 'batch'))
The draws below stay inside these ranges and needn't reach their ends.
Inputs may be any that keep to these rules, and one draw needn't show every extreme that they name: `query_cluster`: among the rows of one device every cluster appears at least once and none more than 4 times; on every device of one batch index one cluster, drawn for that index, appears exactly 4 times. `store_counts`: at least one cluster has all 2048 rows live.
All inputs are finite; a program needn't handle non-finite values.
Results may differ from the reference program's by a relative error of at most 0.0008.
Values may be sent and summed in bfloat16 or wider, within the bound.
No kernel may reach another device: no remote copies, remote signals or barrier semaphores. Data moves between devices by JAX's collectives and lax.ppermute only.
A program may use at most 64 MiB of HBM per device.

```python
import math
import jax
import jax.numpy as jnp
from jax import lax

D = 1152
DEVICE_NEW_ROWS = 128
CROWS = 2048
CLUSTERS = 64
MOST = 4
N_STORE = 64
N_BATCH = 4


def layout_counts(key):
    counts_base = jax.random.randint(jax.random.fold_in(key, 11), (CLUSTERS,), 2, CROWS + 1)
    heavy_one = jax.random.randint(jax.random.fold_in(key, 12), (), 0, CLUSTERS)
    return counts_base.at[heavy_one].set(CROWS).astype(jnp.int32)


def layout_clusters(key):
    devices = N_STORE * N_BATCH
    heavy_ones = jax.random.randint(jax.random.fold_in(key, 21), (N_BATCH,), 0, CLUSTERS)
    slots = jnp.arange(CLUSTERS * MOST, dtype=jnp.int32)
    holder = slots // MOST

    def single_accelerator(position):
        dev_key = jax.random.fold_in(jax.random.fold_in(key, 22), position)
        heavy = heavy_ones[position % N_BATCH]
        needed = (slots % MOST == 0) | (holder == heavy)
        shuffle_order = jax.random.permutation(jax.random.fold_in(dev_key, 1), CLUSTERS * MOST).astype(jnp.int32)
        priority = jnp.where(needed, slots, CLUSTERS * MOST + shuffle_order)
        chosen = jnp.argsort(priority)[:DEVICE_NEW_ROWS]
        picked = holder[chosen]
        return picked[jax.random.permutation(jax.random.fold_in(dev_key, 2), DEVICE_NEW_ROWS)]
    every = jax.vmap(single_accelerator)(jnp.arange(devices, dtype=jnp.int32))
    return every.reshape(devices * DEVICE_NEW_ROWS).astype(jnp.int32)


def centroids(key):
    return jax.random.normal(jax.random.fold_in(key, 31), (CLUSTERS, D), jnp.float32)


def store_row(key, centres, position):
    centre = centres[position // CROWS]
    own_noise = jax.random.normal(jax.random.fold_in(jax.random.fold_in(key, 32), position), (D,), jnp.float32)
    row_value = 0.7 * centre + own_noise
    return jnp.clip(row_value, -6.0, 6.0)


def draw_store(key, part):
    centres = centroids(key)

    def make_row(position):
        return store_row(key, centres, position)
    return jax.vmap(make_row)(jnp.arange(CLUSTERS * CROWS, dtype=jnp.int32)).astype(jnp.bfloat16)


def draw_store_counts(key, part):
    return layout_counts(key)


def draw_query_cluster(key, part):
    return layout_clusters(key)


def draw_queries(key, part):
    centres = centroids(key)
    labels = layout_clusters(key)
    row_total = labels.shape[0]
    rise = 0.4 + 1.6 * jnp.arange(row_total, dtype=jnp.float32) / row_total
    noise_rows = jax.random.normal(jax.random.fold_in(key, 41), (row_total, D), jnp.float32)
    rows_out = 0.7 * rise[:, None] * centres[labels] + noise_rows
    return jnp.clip(rows_out, -6.0, 6.0).astype(jnp.bfloat16)


def setup_inputs(seed: int = 0) -> dict:
    arg_keys = jax.random.split(jax.random.key(seed), 5)
    return {
        "queries": draw_queries(jax.random.fold_in(arg_keys[4], 71), 0),
        "query_cluster": draw_query_cluster(jax.random.fold_in(arg_keys[4], 71), 0),
        "store": draw_store(jax.random.fold_in(arg_keys[4], 71), 0),
        "store_counts": draw_store_counts(jax.random.fold_in(arg_keys[4], 71), 0),
    }


normalized_sharpness = 160.0
epsilon = 1e-06

def inverse_norms(block_of):
    wide = block_of.astype(jnp.float32)
    return lax.rsqrt(lax.optimization_barrier(jnp.sum(wide * wide, axis=1)) + epsilon)

def score_all(queries_in, block_of, scale_part, live_count):
    queries_scale = inverse_norms(queries_in)
    active_indicator = jnp.arange(block_of.shape[0], dtype=jnp.int32) < live_count
    raw_dot = jnp.dot(queries_in, block_of.T, preferred_element_type=jnp.float32)
    angular_similarity = jnp.where(active_indicator[None, :], raw_dot * queries_scale[:, None] * scale_part[None, :], -2.0)
    foremost_couple = lax.top_k(angular_similarity, 2)[0]
    exponential_summands = jnp.where(active_indicator[None, :], jnp.exp(normalized_sharpness * (angular_similarity - foremost_couple[:, :1])), 0.0)
    exp_total = lax.optimization_barrier(jnp.sum(exponential_summands, axis=1))
    weighted = jnp.dot(exponential_summands.astype(jnp.bfloat16), block_of, preferred_element_type=jnp.float32)
    return (weighted / exp_total[:, None], foremost_couple)

def reference(queries, query_cluster, store, store_counts):
    total_rows, features = queries.shape
    clusters = store_counts.shape[0]
    region = store.shape[0] // clusters
    capacity = N_STORE * N_BATCH * MOST
    labels = jnp.arange(clusters, dtype=jnp.int32)
    members = lax.optimization_barrier(jnp.sum((query_cluster[None, :] == labels[:, None]).astype(jnp.int32), axis=1)).astype(jnp.int32)
    starts = (jnp.cumsum(members) - members).astype(jnp.int32)
    sorted_rows = jnp.argsort(query_cluster, stable=True).astype(jnp.int32)
    slot_ids = jnp.arange(capacity, dtype=jnp.int32)

    def one_cluster(label):
        block_of = lax.dynamic_slice_in_dim(store, (label * region).astype(jnp.int32), region, 0)
        position = jnp.minimum(starts[label] + slot_ids, total_rows - 1).astype(jnp.int32)
        occupied = slot_ids < members[label]
        target = jnp.where(occupied, sorted_rows[position], total_rows).astype(jnp.int32)
        gathered = queries[jnp.minimum(target, total_rows - 1)]
        near, foremost_couple = score_all(gathered, block_of, inverse_norms(block_of), store_counts[label])
        return (target, near, foremost_couple)
    target, near, foremost_couple = lax.map(one_cluster, labels)
    flat_target = target.reshape(-1)
    best_two = jnp.zeros((total_rows, 2), jnp.float32).at[flat_target].set(foremost_couple.reshape(-1, 2), mode='drop')
    neighbours = jnp.zeros((total_rows, features), jnp.float32).at[flat_target].set(near.reshape(-1, features), mode='drop')
    top_cos = best_two[:, 0]
    recency = jnp.exp(jnp.arange(total_rows, dtype=jnp.int32).astype(jnp.float32) * (math.log(3.0) / total_rows))
    totals = jax.ops.segment_sum(recency * top_cos, query_cluster, num_segments=clusters)
    weights = jax.ops.segment_sum(recency, query_cluster, num_segments=clusters)
    cluster_ratio = totals / weights
    novelty = top_cos - cluster_ratio[query_cluster]
    return (best_two, novelty, neighbours)
```

```python
import math

import jax
import jax.numpy as jnp
from jax import lax
from jax.sharding import PartitionSpec as P

normalized_sharpness = 160.0
epsilon = 1e-06
EXTRA = 128
ROW_SCALE = 8192.0
LOW_SCALE = 4096.0


def inverse_norms(block_of):
    wide = block_of.astype(jnp.float32)
    return lax.rsqrt(jnp.sum(wide * wide, axis=1) + epsilon)


def leading_pair(values):
    first = jnp.max(values, axis=1)
    equal_count = jnp.sum((values == first[:, None]).astype(jnp.int32), axis=1)
    below = jnp.max(jnp.where(values < first[:, None], values, -3.0), axis=1)
    second = jnp.where(equal_count >= 2, first, below)
    return first, second


def split_parts(value):
    high = lax.reduce_precision(value, 5, 10)
    low = (value - high) * LOW_SCALE
    return high.astype(jnp.float16), low.astype(jnp.float16)


def over_batch(value):
    n = lax.axis_size("batch")
    total = value
    for k in range(1, n):
        total = total + lax.ppermute(value, "batch", [(i, (i + k) % n) for i in range(n)])
    return total


def body(queries, query_cluster, store, store_counts):
    n_store = lax.axis_size("store")
    n_batch = lax.axis_size("batch")
    rows_dev, features = queries.shape
    clusters = store_counts.shape[0]
    crows = store.shape[0]
    slot_depth = 2 * rows_dev // clusters
    slots = clusters * slot_depth
    total_rows = rows_dev * n_store * n_batch
    growth = math.log(3.0) / total_rows

    local_index = lax.iota(jnp.int32, rows_dev)
    earlier = (query_cluster[:, None] == query_cluster[None, :]) & (
        local_index[None, :] < local_index[:, None]
    )
    rank_in = jnp.sum(earlier.astype(jnp.int32), axis=1)
    slot_of = query_cluster * slot_depth + rank_in

    lane = lax.iota(jnp.int32, EXTRA)
    tail = jnp.where(
        lane[None, :] == 0,
        local_index.astype(jnp.bfloat16)[:, None],
        jnp.where(lane[None, :] == 1, 1.0, 0.0).astype(jnp.bfloat16),
    )
    wide_rows = jnp.concatenate([queries, tail], axis=1)
    place = (lax.iota(jnp.int32, slots)[:, None] == slot_of[None, :]).astype(jnp.bfloat16)
    send_rows = jnp.dot(place, wide_rows, preferred_element_type=jnp.float32)
    send_rows = send_rows.astype(jnp.bfloat16).reshape(clusters, slot_depth, features + EXTRA)

    live_count = store_counts[lax.axis_index("store")]
    store_scale = inverse_norms(store)
    got = lax.all_to_all(send_rows, "store", split_axis=0, concat_axis=0, tiled=True)
    got = got.reshape(slots, features + EXTRA)
    rows = got[:, :features]
    position = got[:, features].astype(jnp.float32)
    taken = got[:, features + 1].astype(jnp.float32)

    active = (lax.iota(jnp.int32, crows) < live_count)[None, :]
    raw_dot = lax.dot_general(
        rows, store, (((1,), (1,)), ((), ())), preferred_element_type=jnp.float32
    )
    cosine = jnp.where(active, raw_dot * inverse_norms(rows)[:, None] * store_scale[None, :], -2.0)
    first, second = leading_pair(cosine)

    source = lax.iota(jnp.int32, slots) // slot_depth
    row_index = (
        ((source * n_batch + lax.axis_index("batch")) * rows_dev).astype(jnp.float32) + position
    )
    recency = jnp.exp(row_index * growth) * taken
    sums = jnp.stack([jnp.sum(recency * first), jnp.sum(recency)])
    sums = over_batch(sums)
    novelty = first - sums[0] / sums[1]

    expo = jnp.where(active, jnp.exp(normalized_sharpness * (cosine - first[:, None])), 0.0)
    weighted = jnp.dot(expo.astype(jnp.bfloat16), store, preferred_element_type=jnp.float32)
    near = weighted * (ROW_SCALE / jnp.sum(expo, axis=1))[:, None]

    parts = [p for v in (first, second, novelty) for p in split_parts(v)]
    parts = jnp.stack(parts + [jnp.zeros_like(parts[0])] * (EXTRA - len(parts)), axis=1)
    back = jnp.concatenate([near.astype(jnp.float16), parts], axis=1)
    back = back.reshape(n_store, slot_depth, features + EXTRA)
    back = lax.all_to_all(back, "store", split_axis=0, concat_axis=0, tiled=True)
    back = back.reshape(slots, features + EXTRA).astype(jnp.float32)

    high = lax.reduce_precision(back, 8, 7)
    low = (back - high).astype(jnp.bfloat16)
    high = high.astype(jnp.bfloat16)
    pick = (slot_of[:, None] == lax.iota(jnp.int32, slots)[None, :]).astype(jnp.bfloat16)
    mine = jnp.dot(pick, high, preferred_element_type=jnp.float32) + jnp.dot(
        pick, low, preferred_element_type=jnp.float32
    )
    neighbours = mine[:, :features] * (1.0 / ROW_SCALE)
    values = mine[:, features : features + 6 : 2] + mine[:, features + 1 : features + 6 : 2] * (
        1.0 / LOW_SCALE
    )
    return (values[:, :2], values[:, 2], neighbours)


def solution(mesh):
    in_specs = (P(("store", "batch"), None), P(("store", "batch")), P("store", None), P())
    out_specs = (P(("store", "batch"), None), P(("store", "batch")), P(("store", "batch"), None))
    return jax.shard_map(body, mesh=mesh, in_specs=in_specs, out_specs=out_specs, check_vma=False)
```

```python
import functools
import math

import jax
import jax.numpy as jnp
from jax import lax
from jax.experimental import pallas as pl
from jax.experimental.pallas import tpu as pltpu
from jax.sharding import PartitionSpec as P

normalized_sharpness = 160.0
epsilon = 1e-06
EXTRA = 128
STEPS = 32767.0
COSINE_UNIT = 16384.0
SUM_UNIT = 32.0
LOG_UNIT = 256.0
LOW_UNIT = 16384.0
TILE = 256
VMEM_BYTES = 24 * 2**20


def dot(a, b, contract):
    return lax.dot_general(a, b, ((contract[:1], contract[1:]), ((), ())), preferred_element_type=jnp.float32)


def cluster_pairs(cluster_ref):
    across = jnp.broadcast_to(cluster_ref[...], (cluster_ref.shape[1],) * 2)
    down = across.T
    i = lax.broadcasted_iota(jnp.int32, across.shape, 0)
    j = lax.broadcasted_iota(jnp.int32, across.shape, 1)
    return across, down, i, j


def place_kernel(depth, cluster_ref, queries_ref, out_ref):
    across, down, i, j = cluster_pairs(cluster_ref)
    rows, features = queries_ref.shape
    rank = jnp.sum(jnp.where((across == down) & (i < j), 1.0, 0.0), axis=0, keepdims=True)
    slot = across[:1] * depth + rank.astype(jnp.int32)
    slots = out_ref.shape[0] * depth
    place = jnp.where(lax.broadcasted_iota(jnp.int32, (slots, rows), 0) == slot, 1.0, 0.0)
    place = place.astype(jnp.bfloat16)
    tail = jnp.where(j == 0, i.astype(jnp.float32), jnp.where(j == 1, 1.0, 0.0))
    sent = dot(place, queries_ref[...], (1, 0)).astype(jnp.bfloat16)
    out_ref[:, :, :features] = sent.reshape(-1, depth, features)
    sent = dot(place, tail.astype(jnp.bfloat16), (1, 0)).astype(jnp.bfloat16)
    out_ref[:, :, features:] = sent.reshape(-1, depth, EXTRA)


def parts(value, unit):
    high = jnp.round(value * unit)
    return [high, jnp.round((value * unit - high) * LOW_UNIT)]


def score_kernel(growth, n_batch, rows_dev, info_ref, got_ref, store_ref, scale_ref, out_ref, cos_ref, expo_ref):
    sources, depth, width = got_ref.shape
    features = width - EXTRA
    slots = sources * depth
    crows = store_ref.shape[0]
    live, batch = info_ref[0], info_ref[1]
    rows = got_ref[:, :, :features].reshape(slots, features)
    tail = got_ref[:, :, features:].astype(jnp.float32).reshape(slots, EXTRA)
    wide = rows.astype(jnp.float32)
    row_scale = lax.rsqrt(jnp.sum(wide * wide, axis=1, keepdims=True) + epsilon)
    lane = lax.broadcasted_iota(jnp.int32, (slots, 128), 1)
    one = jnp.full((slots, 128), -3.0, jnp.float32)
    two = one
    for t in range(crows // TILE):
        raw = dot(rows, store_ref[t * TILE : (t + 1) * TILE, :], (1, 1))
        for h in range(TILE // 128):
            at = t * TILE + h * 128
            cosine = raw[:, h * 128 : (h + 1) * 128] * row_scale * scale_ref[:, at : at + 128]
            cosine = jnp.where(lane < live - at, cosine, -2.0)
            cos_ref[:, at : at + 128] = cosine
            two = jnp.maximum(two, jnp.minimum(one, cosine))
            one = jnp.maximum(one, cosine)
    first = jnp.max(one, axis=1, keepdims=True)
    holder = jnp.min(jnp.where(one == first, lane, 128), axis=1, keepdims=True)
    second = jnp.max(jnp.where(lane == holder, two, one), axis=1, keepdims=True)

    total = jnp.zeros((slots, 128), jnp.float32)
    for at in range(0, crows, 128):
        expo = jnp.exp(normalized_sharpness * (cos_ref[:, at : at + 128] - first))
        expo = jnp.where(lane < live - at, expo, 0.0)
        total = total + expo
        expo_ref[:, at : at + 128] = expo.astype(jnp.bfloat16)
    total = jnp.sum(total, axis=1, keepdims=True)
    weighted = dot(expo_ref[...], store_ref[...], (1, 0))
    largest = jnp.maximum(jnp.max(jnp.abs(weighted), axis=1, keepdims=True), 1e-30)
    coded = jnp.round(weighted * (STEPS / largest)).astype(jnp.int32)
    out_ref[:, :, :features] = coded.reshape(sources, depth, features).astype(jnp.int16)

    slot = lax.broadcasted_iota(jnp.int32, (slots, 1), 0)
    index = (slot // depth * n_batch + batch) * rows_dev + tail[:, :1].astype(jnp.int32)
    recency = jnp.exp(index.astype(jnp.float32) * growth) * tail[:, 1:2]
    values = (
        parts(first, COSINE_UNIT)
        + parts(second, COSINE_UNIT)
        + parts(jnp.log(largest / total), LOG_UNIT)
        + parts(jnp.sum(recency * first, axis=0, keepdims=True), SUM_UNIT)
        + parts(jnp.sum(recency, axis=0, keepdims=True), SUM_UNIT)
    )
    extra = jnp.zeros((slots, 128), jnp.float32)
    for k, value in enumerate(values):
        extra = jnp.where(lane == k, value, extra)
    out_ref[:, :, features:] = extra.astype(jnp.int32).reshape(sources, depth, EXTRA).astype(jnp.int16)


def joined(high, low, unit):
    return (high + low * (1.0 / LOW_UNIT)) * (1.0 / unit)


def pick_kernel(cluster_ref, back_ref, near_ref, best_ref):
    across, down, i, j = cluster_pairs(cluster_ref)
    clusters, depth, width = back_ref.shape
    features = width - EXTRA
    slots = clusters * depth
    rank = jnp.sum(jnp.where((across == down) & (j < i), 1.0, 0.0), axis=1, keepdims=True)
    slot = down[:, :1] * depth + rank.astype(jnp.int32)
    pick = jnp.where(lax.broadcasted_iota(jnp.int32, (i.shape[0], slots), 1) == slot, 1.0, 0.0)
    pick = pick.astype(jnp.bfloat16)

    def mine(value):
        value = value.astype(jnp.float32).reshape(slots, -1)
        high = jnp.floor(value * (1.0 / 256.0))
        low = value - high * 256.0
        return dot(pick, high.astype(jnp.bfloat16), (1, 0)) * 256.0 + dot(pick, low.astype(jnp.bfloat16), (1, 0))

    extra = mine(back_ref[:, :, features:])
    largest = jnp.exp(joined(extra[:, 4:5], extra[:, 5:6], LOG_UNIT))
    near_ref[...] = mine(back_ref[:, :, :features]) * (largest * (1.0 / STEPS))
    extra = extra.T
    best_ref[0:1, :] = joined(extra[0:1], extra[1:2], COSINE_UNIT)
    best_ref[1:2, :] = joined(extra[2:3], extra[3:4], COSINE_UNIT)


def over_batch(value):
    n = lax.axis_size("batch")
    total = value
    for k in range(1, n):
        total = total + lax.ppermute(value, "batch", [(i, (i + k) % n) for i in range(n)])
    return total


def inverse_norms(block_of):
    wide = block_of.astype(jnp.float32)
    return lax.rsqrt(jnp.sum(wide * wide, axis=1) + epsilon)


def body(queries, query_cluster, store, store_counts):
    n_store = lax.axis_size("store")
    n_batch = lax.axis_size("batch")
    rows_dev, features = queries.shape
    clusters = store_counts.shape[0]
    crows = store.shape[0]
    depth = 2 * rows_dev // clusters
    slots = clusters * depth
    width = features + EXTRA
    growth = math.log(3.0) / (rows_dev * n_store * n_batch)
    params = pltpu.CompilerParams(vmem_limit_bytes=VMEM_BYTES)

    cluster_row = query_cluster.reshape(1, rows_dev)
    send = pl.pallas_call(
        functools.partial(place_kernel, depth),
        out_shape=jax.ShapeDtypeStruct((clusters, depth, width), jnp.bfloat16),
        compiler_params=params,
    )(cluster_row, queries)

    info = jnp.stack([store_counts[lax.axis_index("store")], lax.axis_index("batch")])
    store_scale = inverse_norms(store).reshape(1, crows)
    got = lax.all_to_all(send, "store", split_axis=0, concat_axis=0, tiled=True)

    vmem = pl.BlockSpec(memory_space=pltpu.VMEM)
    back = pl.pallas_call(
        functools.partial(score_kernel, growth, n_batch, rows_dev),
        out_shape=jax.ShapeDtypeStruct((n_store, depth, width), jnp.int16),
        in_specs=[pl.BlockSpec(memory_space=pltpu.SMEM), vmem, vmem, vmem],
        out_specs=vmem,
        scratch_shapes=[pltpu.VMEM((slots, crows), jnp.float32), pltpu.VMEM((slots, crows), jnp.bfloat16)],
        compiler_params=params,
    )(info, got, store, store_scale)
    back = lax.all_to_all(back, "store", split_axis=0, concat_axis=0, tiled=True)

    sums = back[:, 0, features + 6 : features + 10].astype(jnp.float32)
    sums = over_batch(joined(sums[:, 0::2], sums[:, 1::2], SUM_UNIT))
    near, best = pl.pallas_call(
        pick_kernel,
        out_shape=(
            jax.ShapeDtypeStruct((rows_dev, features), jnp.float32),
            jax.ShapeDtypeStruct((2, rows_dev), jnp.float32),
        ),
        compiler_params=params,
    )(cluster_row, back)
    mean = sums[:, 0] / sums[:, 1]
    member = query_cluster[:, None] == lax.iota(jnp.int32, clusters)[None, :]
    novelty = best[0] - jnp.sum(jnp.where(member, mean[None, :], 0.0), axis=1)
    return (best.T, novelty, near)


def solution(mesh):
    in_specs = (P(("store", "batch"), None), P(("store", "batch")), P("store", None), P())
    out_specs = (P(("store", "batch"), None), P(("store", "batch")), P(("store", "batch"), None))
    return jax.shard_map(body, mesh=mesh, in_specs=in_specs, out_specs=out_specs, check_vma=False)
```

```python
import functools
import math

import jax
import jax.numpy as jnp
from jax import lax
from jax.experimental import pallas as pl
from jax.experimental.pallas import tpu as pltpu
from jax.sharding import PartitionSpec as P

normalized_sharpness = 160.0
epsilon = 1e-06
EXTRA = 128
STEPS = 32767.0
COSINE_UNIT = 16384.0
NOVELTY_UNIT = 8192.0
LOG_UNIT = 256.0
LOW_UNIT = 16384.0
TILE = 256
VMEM_BYTES = 24 * 2**20


def dot(a, b, contract):
    return lax.dot_general(a, b, ((contract[:1], contract[1:]), ((), ())), preferred_element_type=jnp.float32)


def cluster_pairs(cluster_ref):
    across = jnp.broadcast_to(cluster_ref[...], (cluster_ref.shape[1],) * 2)
    down = across.T
    i = lax.broadcasted_iota(jnp.int32, across.shape, 0)
    j = lax.broadcasted_iota(jnp.int32, across.shape, 1)
    return across, down, i, j


def place_kernel(depth, cluster_hbm, queries_hbm, out_ref, cluster_ref, queries_ref, cluster_sem, queries_sem):
    copy_cluster = pltpu.make_async_copy(cluster_hbm, cluster_ref, cluster_sem)
    copy_queries = pltpu.make_async_copy(queries_hbm, queries_ref, queries_sem)
    copy_cluster.start()
    copy_queries.start()
    copy_cluster.wait()
    across, down, i, j = cluster_pairs(cluster_ref)
    rows, features = queries_ref.shape
    rank = jnp.sum(jnp.where((across == down) & (i < j), 1.0, 0.0), axis=0, keepdims=True)
    slot = across[:1] * depth + rank.astype(jnp.int32)
    slots = out_ref.shape[0] * depth
    place = jnp.where(lax.broadcasted_iota(jnp.int32, (slots, rows), 0) == slot, 1.0, 0.0)
    place = place.astype(jnp.bfloat16)
    tail = jnp.where(j == 0, i.astype(jnp.float32), jnp.where(j == 1, 1.0, 0.0))
    sent = dot(place, tail.astype(jnp.bfloat16), (1, 0)).astype(jnp.bfloat16)
    out_ref[:, :, features:] = sent.reshape(-1, depth, EXTRA)
    copy_queries.wait()
    sent = dot(place, queries_ref[...], (1, 0)).astype(jnp.bfloat16)
    out_ref[:, :, :features] = sent.reshape(-1, depth, features)


def scale_kernel(store_hbm, scale_ref, near_ref, rest_ref, near_sem, rest_sem):
    near = near_ref.shape[0]
    copies = [
        pltpu.make_async_copy(store_hbm.at[pl.ds(0, near)], near_ref, near_sem),
        pltpu.make_async_copy(store_hbm.at[pl.ds(near, rest_ref.shape[0])], rest_ref, rest_sem),
    ]
    for copy in copies:
        copy.start()
    for copy, held, base in zip(copies, (near_ref, rest_ref), (0, near)):
        copy.wait()
        for at in range(0, held.shape[0], 128):
            wide = held[at : at + 128, :].astype(jnp.float32)
            wide = wide * wide
            total = wide[:, :128]
            for k in range(128, wide.shape[1], 128):
                total = total + wide[:, k : k + 128]
            total = jnp.sum(total.T, axis=0, keepdims=True)
            scale_ref[:, base + at : base + at + 128] = lax.rsqrt(total + epsilon)


def parts(value, unit):
    high = jnp.round(value * unit)
    return [high, jnp.round((value * unit - high) * LOW_UNIT)]


def cosines(rows, row_scale, held_ref, scale_ref, live, base, one, two, cos_ref):
    lane = lax.broadcasted_iota(jnp.int32, one.shape, 1)
    for t in range(0, held_ref.shape[0], TILE):
        raw = dot(rows, held_ref[t : t + TILE, :], (1, 1))
        for h in range(0, TILE, 128):
            at = t + h
            cosine = raw[:, h : h + 128] * row_scale * scale_ref[:, base + at : base + at + 128]
            cosine = jnp.where(lane < live - base - at, cosine, -2.0)
            cos_ref[:, at : at + 128] = cosine
            two = jnp.maximum(two, jnp.minimum(one, cosine))
            one = jnp.maximum(one, cosine)
    return one, two


def near_kernel(info_ref, got_ref, near_ref, scale_ref, cos_ref, rows_ref, state_ref):
    sources, depth, width = got_ref.shape
    slots, features = sources * depth, width - EXTRA
    rows_ref[...] = got_ref[...].reshape(slots, width)
    rows = rows_ref[:, :features]
    wide = rows.astype(jnp.float32)
    row_scale = lax.rsqrt(jnp.sum(wide * wide, axis=1, keepdims=True) + epsilon)
    state_ref[0] = jnp.broadcast_to(row_scale, (slots, 128))
    one = jnp.full((slots, 128), -3.0, jnp.float32)
    state_ref[1], state_ref[2] = cosines(rows, row_scale, near_ref, scale_ref, info_ref[0], 0, one, one, cos_ref)


def rest_kernel(
    growth, n_batch, rows_dev, depth, info_ref, rows_ref, state_ref, rest_ref, scale_ref, cos_ref, best_ref, sums_ref
):
    slots, width = rows_ref.shape
    features = width - EXTRA
    live, batch = info_ref[0], info_ref[1]
    tail = rows_ref[:, features:].astype(jnp.float32)
    slot = lax.broadcasted_iota(jnp.int32, (slots, 1), 0)
    index = (slot // depth * n_batch + batch) * rows_dev + tail[:, :1].astype(jnp.int32)
    recency = jnp.exp(index.astype(jnp.float32) * growth) * tail[:, 1:2]
    base = scale_ref.shape[1] - rest_ref.shape[0]
    one, two = cosines(
        rows_ref[:, :features], state_ref[0][:, :1], rest_ref, scale_ref, live, base, state_ref[1], state_ref[2], cos_ref
    )
    lane = lax.broadcasted_iota(jnp.int32, (slots, 128), 1)
    first = jnp.max(one, axis=1, keepdims=True)
    holder = jnp.min(jnp.where(one == first, lane, 128), axis=1, keepdims=True)
    second = jnp.max(jnp.where(lane == holder, two, one), axis=1, keepdims=True)
    best_ref[...] = jnp.where(lane == 0, first, second)
    across = lax.broadcasted_iota(jnp.int32, sums_ref.shape, 1)
    sums_ref[...] = jnp.where(
        across == 0,
        jnp.sum(recency * first, axis=0, keepdims=True),
        jnp.sum(recency, axis=0, keepdims=True),
    )


def weigh_kernel(info_ref, cos_near_ref, cos_rest_ref, best_ref, near_ref, rest_ref, weighted_ref, total_ref, expo_ref):
    slots, near = cos_near_ref.shape
    live = info_ref[0]
    first = best_ref[:, :1]
    lane = lax.broadcasted_iota(jnp.int32, (slots, 128), 1)
    total = jnp.zeros((slots, 128), jnp.float32)
    for cos_ref, base in ((cos_near_ref, 0), (cos_rest_ref, near)):
        for at in range(0, cos_ref.shape[1], 128):
            expo = jnp.exp(normalized_sharpness * (cos_ref[:, at : at + 128] - first))
            expo = jnp.where(lane < live - base - at, expo, 0.0)
            total = total + expo
            expo_ref[:, base + at : base + at + 128] = expo.astype(jnp.bfloat16)
    total_ref[...] = total
    weighted = dot(expo_ref[:, :near], near_ref[...], (1, 0))
    weighted_ref[...] = weighted + dot(expo_ref[:, near:], rest_ref[...], (1, 0))


def code_kernel(weighted_ref, total_ref, best_ref, *refs):
    *sums_refs, out_ref = refs
    sources, depth, width = out_ref.shape
    features = width - EXTRA
    slots = sources * depth
    sums = sums_refs[0][...]
    for ref in sums_refs[1:]:
        sums = sums + ref[...]
    mean = sums[:, :1] / sums[:, 1:2]
    first, second = best_ref[:, :1], best_ref[:, 1:2]
    total = jnp.sum(total_ref[...], axis=1, keepdims=True)
    weighted = weighted_ref[...]
    largest = jnp.maximum(jnp.max(jnp.abs(weighted), axis=1, keepdims=True), 1e-30)
    coded = jnp.round(weighted * (STEPS / largest)).astype(jnp.int32)
    out_ref[:, :, :features] = coded.reshape(sources, depth, features).astype(jnp.int16)
    values = (
        parts(first, COSINE_UNIT)
        + parts(second, COSINE_UNIT)
        + parts(jnp.log(largest / total), LOG_UNIT)
        + parts(first - mean, NOVELTY_UNIT)
    )
    lane = lax.broadcasted_iota(jnp.int32, (slots, 128), 1)
    extra = jnp.zeros((slots, 128), jnp.float32)
    for k, value in enumerate(values):
        extra = jnp.where(lane == k, value, extra)
    out_ref[:, :, features:] = extra.astype(jnp.int32).reshape(sources, depth, EXTRA).astype(jnp.int16)


def joined(high, low, unit):
    return (high + low * (1.0 / LOW_UNIT)) * (1.0 / unit)


def pick_kernel(cluster_ref, back_ref, near_ref, best_ref, novelty_ref):
    across, down, i, j = cluster_pairs(cluster_ref)
    clusters, depth, width = back_ref.shape
    features = width - EXTRA
    slots = clusters * depth
    rank = jnp.sum(jnp.where((across == down) & (j < i), 1.0, 0.0), axis=1, keepdims=True)
    slot = down[:, :1] * depth + rank.astype(jnp.int32)
    pick = jnp.where(lax.broadcasted_iota(jnp.int32, (i.shape[0], slots), 1) == slot, 1.0, 0.0)
    pick = pick.astype(jnp.bfloat16)

    def mine(value):
        value = value.astype(jnp.float32).reshape(slots, -1)
        high = jnp.floor(value * (1.0 / 256.0))
        low = value - high * 256.0
        return dot(pick, high.astype(jnp.bfloat16), (1, 0)) * 256.0 + dot(pick, low.astype(jnp.bfloat16), (1, 0))

    extra = mine(back_ref[:, :, features:])
    largest = jnp.exp(joined(extra[:, 4:5], extra[:, 5:6], LOG_UNIT))
    near_ref[...] = mine(back_ref[:, :, :features]) * (largest * (1.0 / STEPS))
    extra = extra.T
    best_ref[0:1, :] = joined(extra[0:1], extra[1:2], COSINE_UNIT)
    best_ref[1:2, :] = joined(extra[2:3], extra[3:4], COSINE_UNIT)
    novelty_ref[...] = joined(extra[6:7], extra[7:8], NOVELTY_UNIT)


def over_batch(value):
    n = lax.axis_size("batch")
    return [value] + [lax.ppermute(value, "batch", [(i, (i + k) % n) for i in range(n)]) for k in range(1, n)]


def body(queries, query_cluster, store, store_counts):
    n_store = lax.axis_size("store")
    n_batch = lax.axis_size("batch")
    rows_dev, features = queries.shape
    clusters = store_counts.shape[0]
    crows = store.shape[0]
    depth = 2 * rows_dev // clusters
    slots = clusters * depth
    width = features + EXTRA
    growth = math.log(3.0) / (rows_dev * n_store * n_batch)
    params = pltpu.CompilerParams(vmem_limit_bytes=VMEM_BYTES)

    cluster_row = query_cluster.reshape(1, rows_dev)
    send = pl.pallas_call(
        functools.partial(place_kernel, depth),
        out_shape=jax.ShapeDtypeStruct((clusters, depth, width), jnp.bfloat16),
        in_specs=[pl.BlockSpec(memory_space=pltpu.HBM)] * 2,
        scratch_shapes=[
            pltpu.VMEM((1, rows_dev), jnp.int32),
            pltpu.VMEM((rows_dev, features), jnp.bfloat16),
            pltpu.SemaphoreType.DMA,
            pltpu.SemaphoreType.DMA,
        ],
        compiler_params=pltpu.CompilerParams(vmem_limit_bytes=60 * 2**20),
    )(cluster_row, queries)

    info = jnp.stack([store_counts[lax.axis_index("store")], lax.axis_index("batch")])
    near = crows // 2
    f32, bf16 = jnp.float32, store.dtype
    vmem = pl.BlockSpec(memory_space=pltpu.VMEM)
    hbm = pl.BlockSpec(memory_space=pltpu.HBM)
    smem = pl.BlockSpec(memory_space=pltpu.SMEM)
    store_scale, store_near, store_rest = pl.pallas_call(
        scale_kernel,
        out_shape=(
            jax.ShapeDtypeStruct((1, crows), f32),
            jax.ShapeDtypeStruct((near, features), bf16),
            jax.ShapeDtypeStruct((crows - near, features), bf16),
        ),
        in_specs=[hbm],
        out_specs=(vmem,) * 3,
        scratch_shapes=[pltpu.SemaphoreType.DMA, pltpu.SemaphoreType.DMA],
        compiler_params=params,
        cost_estimate=pl.CostEstimate(flops=2 * crows * features, bytes_accessed=2 * crows * features, transcendentals=crows),
    )(store)
    got = lax.all_to_all(send, "store", split_axis=0, concat_axis=0, tiled=True)

    half_cost = pl.CostEstimate(flops=slots * crows * features, bytes_accessed=crows * features, transcendentals=0)
    cos_near, rows, state = pl.pallas_call(
        near_kernel,
        out_shape=(
            jax.ShapeDtypeStruct((slots, near), f32),
            jax.ShapeDtypeStruct((slots, width), bf16),
            jax.ShapeDtypeStruct((3, slots, 128), f32),
        ),
        in_specs=[smem, vmem, vmem, vmem],
        out_specs=(vmem,) * 3,
        compiler_params=params,
        cost_estimate=half_cost,
    )(info, got, store_near, store_scale)
    cos_rest, best, sums = pl.pallas_call(
        functools.partial(rest_kernel, growth, n_batch, rows_dev, depth),
        out_shape=(
            jax.ShapeDtypeStruct((slots, crows - near), f32),
            jax.ShapeDtypeStruct((slots, 128), f32),
            jax.ShapeDtypeStruct((1, 128), f32),
        ),
        in_specs=[smem, vmem, vmem, vmem, vmem],
        out_specs=(vmem,) * 3,
        compiler_params=params,
        cost_estimate=half_cost,
    )(info, rows, state, store_rest, store_scale)
    sums = over_batch(sums)
    weighted, total = pl.pallas_call(
        weigh_kernel,
        out_shape=(
            jax.ShapeDtypeStruct((slots, features), jnp.float32),
            jax.ShapeDtypeStruct((slots, 128), jnp.float32),
        ),
        in_specs=[smem] + [vmem] * 5,
        out_specs=(vmem, vmem),
        scratch_shapes=[pltpu.VMEM((slots, crows), jnp.bfloat16)],
        compiler_params=params,
        cost_estimate=pl.CostEstimate(flops=4 * slots * crows * features, bytes_accessed=8 * crows * features, transcendentals=slots * crows),
    )(info, cos_near, cos_rest, best, store_near, store_rest)
    back = pl.pallas_call(
        code_kernel,
        out_shape=jax.ShapeDtypeStruct((n_store, depth, width), jnp.int16),
        in_specs=[vmem] * (3 + n_batch),
        out_specs=vmem,
        compiler_params=params,
    )(weighted, total, best, *sums)
    back = lax.all_to_all(back, "store", split_axis=0, concat_axis=0, tiled=True)

    neighbours, best, novelty = pl.pallas_call(
        pick_kernel,
        out_shape=(
            jax.ShapeDtypeStruct((rows_dev, features), jnp.float32),
            jax.ShapeDtypeStruct((2, rows_dev), jnp.float32),
            jax.ShapeDtypeStruct((1, rows_dev), jnp.float32),
        ),
        compiler_params=params,
    )(cluster_row, back)
    return (best.T, novelty[0], neighbours)


def solution(mesh):
    in_specs = (P(("store", "batch"), None), P(("store", "batch")), P("store", None), P())
    out_specs = (P(("store", "batch"), None), P(("store", "batch")), P(("store", "batch"), None))
    return jax.shard_map(body, mesh=mesh, in_specs=in_specs, out_specs=out_specs, check_vma=False)
```

```python
import functools
import math

import jax
import jax.numpy as jnp
from jax import lax
from jax.experimental import pallas as pl
from jax.experimental.pallas import tpu as pltpu
from jax.sharding import PartitionSpec as P

normalized_sharpness = 160.0
epsilon = 1e-06
EXTRA = 128
SIDE = 2
STEPS = 32767.0
COSINE_UNIT = 16384.0
NOVELTY_UNIT = 8192.0
LOG_UNIT = 256.0
LOW_UNIT = 16384.0
TILE = 256
VMEM_BYTES = 24 * 2**20


def dot(a, b, contract):
    return lax.dot_general(a, b, ((contract[:1], contract[1:]), ((), ())), preferred_element_type=jnp.float32)


def slot_of(cluster, rank, clusters):
    return rank // 2 * (2 * clusters) + cluster * 2 + rank % 2


def shifted(value, count):
    return jnp.concatenate([value[:, -count:], value[:, :-count]], axis=1) if count else value


def cluster_pairs(cluster_ref):
    across = jnp.broadcast_to(cluster_ref[...], (cluster_ref.shape[1],) * 2)
    down = across.T
    i = lax.broadcasted_iota(jnp.int32, across.shape, 0)
    j = lax.broadcasted_iota(jnp.int32, across.shape, 1)
    return across, down, i, j


def place_kernel(cluster_hbm, queries_hbm, out_ref, cluster_ref, queries_ref, cluster_sem, queries_sem):
    copy_cluster = pltpu.make_async_copy(cluster_hbm, cluster_ref, cluster_sem)
    copy_queries = pltpu.make_async_copy(queries_hbm, queries_ref, queries_sem)
    copy_cluster.start()
    copy_queries.start()
    copy_cluster.wait()
    across, down, i, j = cluster_pairs(cluster_ref)
    rows, features = queries_ref.shape
    clusters, pair, _ = out_ref.shape
    rank = jnp.sum(jnp.where((across == down) & (i < j), 1.0, 0.0), axis=0, keepdims=True)
    slot = slot_of(across[:1], rank.astype(jnp.int32), clusters)
    step = clusters * pair
    place = jnp.where(lax.broadcasted_iota(jnp.int32, (SIDE * step, rows), 0) == slot, 1.0, 0.0)
    place = place.astype(jnp.bfloat16)
    extra = jnp.zeros((step, EXTRA), jnp.float32)
    for h in range(SIDE):
        at = h * (EXTRA // SIDE)
        tail = jnp.where(j == at, i.astype(jnp.float32), jnp.where(j == at + 1, 1.0, 0.0))
        extra = extra + dot(place[h * step : (h + 1) * step], tail.astype(jnp.bfloat16), (1, 0))
    out_ref[:, :, SIDE * features :] = extra.astype(jnp.bfloat16).reshape(clusters, pair, EXTRA)
    copy_queries.wait()
    for h in range(SIDE):
        sent = dot(place[h * step : (h + 1) * step], queries_ref[...], (1, 0)).astype(jnp.bfloat16)
        out_ref[:, :, h * features : (h + 1) * features] = sent.reshape(clusters, pair, features)


def scale_kernel(store_hbm, scale_ref, near_ref, rest_ref, near_sem, rest_sem):
    near = near_ref.shape[0]
    copies = [
        pltpu.make_async_copy(store_hbm.at[pl.ds(0, near)], near_ref, near_sem),
        pltpu.make_async_copy(store_hbm.at[pl.ds(near, rest_ref.shape[0])], rest_ref, rest_sem),
    ]
    for copy in copies:
        copy.start()
    for copy, held, base in zip(copies, (near_ref, rest_ref), (0, near)):
        copy.wait()
        for at in range(0, held.shape[0], 128):
            wide = held[at : at + 128, :].astype(jnp.float32)
            wide = wide * wide
            total = wide[:, :128]
            for k in range(128, wide.shape[1], 128):
                total = total + wide[:, k : k + 128]
            total = jnp.sum(total.T, axis=0, keepdims=True)
            scale_ref[:, base + at : base + at + 128] = lax.rsqrt(total + epsilon)


def parts(value, unit):
    high = jnp.round(value * unit)
    return [high, jnp.round((value * unit - high) * LOW_UNIT)]


def cosines(rows, row_scale, held_ref, scale_ref, live, base, one, two, cos_ref):
    lane = lax.broadcasted_iota(jnp.int32, one.shape, 1)
    for t in range(0, held_ref.shape[0], TILE):
        raw = dot(rows, held_ref[t : t + TILE, :], (1, 1))
        for h in range(0, TILE, 128):
            at = t + h
            cosine = raw[:, h : h + 128] * row_scale * scale_ref[:, base + at : base + at + 128]
            cosine = jnp.where(lane < live - base - at, cosine, -2.0)
            cos_ref[:, at : at + 128] = cosine
            two = jnp.maximum(two, jnp.minimum(one, cosine))
            one = jnp.maximum(one, cosine)
    return one, two


def near_kernel(info_ref, got_ref, near_ref, scale_ref, cos_ref, rows_ref, state_ref):
    sources, pair, width = got_ref.shape
    features = (width - EXTRA) // SIDE
    step = sources * pair
    slots = SIDE * step
    extra = got_ref[:, :, SIDE * features :].reshape(step, EXTRA).astype(jnp.float32)
    for h in range(SIDE):
        span = slice(h * step, (h + 1) * step)
        rows_ref[span, :features] = got_ref[:, :, h * features : (h + 1) * features].reshape(step, features)
        rows_ref[span, features:] = shifted(extra, h * (EXTRA // SIDE)).astype(rows_ref.dtype)
    rows = rows_ref[:, :features]
    wide = rows.astype(jnp.float32)
    row_scale = lax.rsqrt(jnp.sum(wide * wide, axis=1, keepdims=True) + epsilon)
    state_ref[0] = jnp.broadcast_to(row_scale, (slots, 128))
    one = jnp.full((slots, 128), -3.0, jnp.float32)
    state_ref[1], state_ref[2] = cosines(rows, row_scale, near_ref, scale_ref, info_ref[0], 0, one, one, cos_ref)


def rest_kernel(
    growth, n_batch, rows_dev, n_store, info_ref, rows_ref, state_ref, rest_ref, scale_ref, cos_ref, best_ref, sums_ref
):
    slots, width = rows_ref.shape
    features = width - EXTRA
    live, batch = info_ref[0], info_ref[1]
    tail = rows_ref[:, features:].astype(jnp.float32)
    slot = lax.broadcasted_iota(jnp.int32, (slots, 1), 0)
    index = (slot % (2 * n_store) // 2 * n_batch + batch) * rows_dev + tail[:, :1].astype(jnp.int32)
    recency = jnp.exp(index.astype(jnp.float32) * growth) * tail[:, 1:2]
    base = scale_ref.shape[1] - rest_ref.shape[0]
    one, two = cosines(
        rows_ref[:, :features], state_ref[0][:, :1], rest_ref, scale_ref, live, base, state_ref[1], state_ref[2], cos_ref
    )
    lane = lax.broadcasted_iota(jnp.int32, (slots, 128), 1)
    first = jnp.max(one, axis=1, keepdims=True)
    holder = jnp.min(jnp.where(one == first, lane, 128), axis=1, keepdims=True)
    second = jnp.max(jnp.where(lane == holder, two, one), axis=1, keepdims=True)
    best_ref[...] = jnp.where(lane == 0, first, second)
    across = lax.broadcasted_iota(jnp.int32, sums_ref.shape, 1)
    sums_ref[...] = jnp.where(
        across == 0,
        jnp.sum(recency * first, axis=0, keepdims=True),
        jnp.sum(recency, axis=0, keepdims=True),
    )


def weigh_kernel(info_ref, cos_near_ref, cos_rest_ref, best_ref, near_ref, rest_ref, weighted_ref, total_ref, expo_ref):
    slots, near = cos_near_ref.shape
    live = info_ref[0]
    first = best_ref[:, :1]
    lane = lax.broadcasted_iota(jnp.int32, (slots, 128), 1)
    total = jnp.zeros((slots, 128), jnp.float32)
    for cos_ref, base in ((cos_near_ref, 0), (cos_rest_ref, near)):
        for at in range(0, cos_ref.shape[1], 128):
            expo = jnp.exp(normalized_sharpness * (cos_ref[:, at : at + 128] - first))
            expo = jnp.where(lane < live - base - at, expo, 0.0)
            total = total + expo
            expo_ref[:, base + at : base + at + 128] = expo.astype(jnp.bfloat16)
    total_ref[...] = total
    weighted = dot(expo_ref[:, :near], near_ref[...], (1, 0))
    weighted_ref[...] = weighted + dot(expo_ref[:, near:], rest_ref[...], (1, 0))


def code_kernel(weighted_ref, total_ref, best_ref, *refs):
    *sums_refs, out_ref = refs
    sources, pair, width = out_ref.shape
    features = (width - EXTRA) // SIDE
    step = sources * pair
    slots = SIDE * step
    sums = sums_refs[0][...]
    for ref in sums_refs[1:]:
        sums = sums + ref[...]
    mean = sums[:, :1] / sums[:, 1:2]
    first, second = best_ref[:, :1], best_ref[:, 1:2]
    total = jnp.sum(total_ref[...], axis=1, keepdims=True)
    weighted = weighted_ref[...]
    largest = jnp.maximum(jnp.max(jnp.abs(weighted), axis=1, keepdims=True), 1e-30)
    coded = jnp.round(weighted * (STEPS / largest)).astype(jnp.int32).astype(jnp.int16)
    for h in range(SIDE):
        part = coded[h * step : (h + 1) * step].reshape(sources, pair, features)
        out_ref[:, :, h * features : (h + 1) * features] = part
    values = (
        parts(first, COSINE_UNIT)
        + parts(second, COSINE_UNIT)
        + parts(jnp.log(largest / total), LOG_UNIT)
        + parts(first - mean, NOVELTY_UNIT)
    )
    lane = lax.broadcasted_iota(jnp.int32, (step, EXTRA), 1)
    extra = jnp.zeros((step, EXTRA), jnp.float32)
    for k, value in enumerate(values):
        for h in range(SIDE):
            extra = jnp.where(lane == k + h * (EXTRA // SIDE), value[h * step : (h + 1) * step], extra)
    extra = extra.astype(jnp.int32).astype(jnp.int16)
    out_ref[:, :, SIDE * features :] = extra.reshape(sources, pair, EXTRA)


def joined(high, low, unit):
    return (high + low * (1.0 / LOW_UNIT)) * (1.0 / unit)


def pick_kernel(cluster_ref, back_ref, near_ref, best_ref, novelty_ref):
    across, down, i, j = cluster_pairs(cluster_ref)
    clusters, pair, width = back_ref.shape
    features = (width - EXTRA) // SIDE
    step = clusters * pair
    rank = jnp.sum(jnp.where((across == down) & (j < i), 1.0, 0.0), axis=1, keepdims=True)
    slot = slot_of(down[:, :1], rank.astype(jnp.int32), clusters)
    pick = jnp.where(lax.broadcasted_iota(jnp.int32, (i.shape[0], SIDE * step), 1) == slot, 1.0, 0.0)
    pick = pick.astype(jnp.bfloat16)

    pick = jnp.concatenate([pick, pick], axis=1)

    def mine(halves):
        value = jnp.concatenate(halves, axis=0).astype(jnp.float32)
        high = jnp.floor(value * (1.0 / 256.0)) * 256.0
        return dot(pick, jnp.concatenate([high, value - high], axis=0).astype(jnp.bfloat16), (1, 0))

    extra = back_ref[:, :, SIDE * features :].reshape(step, EXTRA).astype(jnp.float32)
    extra = mine([shifted(extra, h * (EXTRA // SIDE)) for h in range(SIDE)])
    largest = jnp.exp(joined(extra[:, 4:5], extra[:, 5:6], LOG_UNIT))
    rows = mine([back_ref[:, :, h * features : (h + 1) * features].reshape(step, features) for h in range(SIDE)])
    near_ref[...] = rows * (largest * (1.0 / STEPS))
    extra = extra.T
    best_ref[0:1, :] = joined(extra[0:1], extra[1:2], COSINE_UNIT)
    best_ref[1:2, :] = joined(extra[2:3], extra[3:4], COSINE_UNIT)
    novelty_ref[...] = joined(extra[6:7], extra[7:8], NOVELTY_UNIT)


def over_batch(value):
    n = lax.axis_size("batch")
    return [value] + [lax.ppermute(value, "batch", [(i, (i + k) % n) for i in range(n)]) for k in range(1, n)]


def body(queries, query_cluster, store, store_counts):
    n_store = lax.axis_size("store")
    n_batch = lax.axis_size("batch")
    rows_dev, features = queries.shape
    clusters = store_counts.shape[0]
    crows = store.shape[0]
    depth = 2 * rows_dev // clusters
    slots = clusters * depth
    pair = depth // SIDE
    width = features + EXTRA
    wide = SIDE * features + EXTRA
    growth = math.log(3.0) / (rows_dev * n_store * n_batch)
    params = pltpu.CompilerParams(vmem_limit_bytes=VMEM_BYTES)

    cluster_row = query_cluster.reshape(1, rows_dev)
    send = pl.pallas_call(
        place_kernel,
        out_shape=jax.ShapeDtypeStruct((clusters, pair, wide), jnp.bfloat16),
        in_specs=[pl.BlockSpec(memory_space=pltpu.HBM)] * 2,
        scratch_shapes=[
            pltpu.VMEM((1, rows_dev), jnp.int32),
            pltpu.VMEM((rows_dev, features), jnp.bfloat16),
            pltpu.SemaphoreType.DMA,
            pltpu.SemaphoreType.DMA,
        ],
        compiler_params=pltpu.CompilerParams(vmem_limit_bytes=60 * 2**20),
    )(cluster_row, queries)

    info = jnp.stack([store_counts[lax.axis_index("store")], lax.axis_index("batch")])
    near = crows // 2
    f32, bf16 = jnp.float32, store.dtype
    vmem = pl.BlockSpec(memory_space=pltpu.VMEM)
    hbm = pl.BlockSpec(memory_space=pltpu.HBM)
    smem = pl.BlockSpec(memory_space=pltpu.SMEM)
    store_scale, store_near, store_rest = pl.pallas_call(
        scale_kernel,
        out_shape=(
            jax.ShapeDtypeStruct((1, crows), f32),
            jax.ShapeDtypeStruct((near, features), bf16),
            jax.ShapeDtypeStruct((crows - near, features), bf16),
        ),
        in_specs=[hbm],
        out_specs=(vmem,) * 3,
        scratch_shapes=[pltpu.SemaphoreType.DMA, pltpu.SemaphoreType.DMA],
        compiler_params=params,
        cost_estimate=pl.CostEstimate(flops=2 * crows * features, bytes_accessed=2 * crows * features, transcendentals=crows),
    )(store)
    got = lax.all_to_all(send, "store", split_axis=0, concat_axis=0, tiled=True)

    half_cost = pl.CostEstimate(flops=slots * crows * features, bytes_accessed=crows * features, transcendentals=0)
    cos_near, rows, state = pl.pallas_call(
        near_kernel,
        out_shape=(
            jax.ShapeDtypeStruct((slots, near), f32),
            jax.ShapeDtypeStruct((slots, width), bf16),
            jax.ShapeDtypeStruct((3, slots, 128), f32),
        ),
        in_specs=[smem, vmem, vmem, vmem],
        out_specs=(vmem,) * 3,
        compiler_params=params,
        cost_estimate=half_cost,
    )(info, got, store_near, store_scale)
    cos_rest, best, sums = pl.pallas_call(
        functools.partial(rest_kernel, growth, n_batch, rows_dev, n_store),
        out_shape=(
            jax.ShapeDtypeStruct((slots, crows - near), f32),
            jax.ShapeDtypeStruct((slots, 128), f32),
            jax.ShapeDtypeStruct((1, 128), f32),
        ),
        in_specs=[smem, vmem, vmem, vmem, vmem],
        out_specs=(vmem,) * 3,
        compiler_params=params,
        cost_estimate=half_cost,
    )(info, rows, state, store_rest, store_scale)
    sums = over_batch(sums)
    weighted, total = pl.pallas_call(
        weigh_kernel,
        out_shape=(
            jax.ShapeDtypeStruct((slots, features), jnp.float32),
            jax.ShapeDtypeStruct((slots, 128), jnp.float32),
        ),
        in_specs=[smem] + [vmem] * 5,
        out_specs=(vmem, vmem),
        scratch_shapes=[pltpu.VMEM((slots, crows), jnp.bfloat16)],
        compiler_params=params,
        cost_estimate=pl.CostEstimate(flops=4 * slots * crows * features, bytes_accessed=8 * crows * features, transcendentals=slots * crows),
    )(info, cos_near, cos_rest, best, store_near, store_rest)
    back = pl.pallas_call(
        code_kernel,
        out_shape=jax.ShapeDtypeStruct((n_store, pair, wide), jnp.int16),
        in_specs=[vmem] * (3 + n_batch),
        out_specs=vmem,
        compiler_params=params,
    )(weighted, total, best, *sums)
    back = lax.all_to_all(back, "store", split_axis=0, concat_axis=0, tiled=True)

    neighbours, best, novelty = pl.pallas_call(
        pick_kernel,
        out_shape=(
            jax.ShapeDtypeStruct((rows_dev, features), jnp.float32),
            jax.ShapeDtypeStruct((2, rows_dev), jnp.float32),
            jax.ShapeDtypeStruct((1, rows_dev), jnp.float32),
        ),
        compiler_params=params,
    )(cluster_row, back)
    return (best.T, novelty[0], neighbours)


def solution(mesh):
    in_specs = (P(("store", "batch"), None), P(("store", "batch")), P("store", None), P())
    out_specs = (P(("store", "batch"), None), P(("store", "batch")), P(("store", "batch"), None))
    return jax.shard_map(body, mesh=mesh, in_specs=in_specs, out_specs=out_specs, check_vma=False)
```

```python
import functools
import math

import jax
import jax.numpy as jnp
from jax import lax
from jax.experimental import pallas as pl
from jax.experimental.pallas import tpu as pltpu
from jax.sharding import PartitionSpec as P

normalized_sharpness = 160.0
epsilon = 1e-06
EXTRA = 128
SIDE = 2
STEPS = 32767.0
COSINE_UNIT = 16384.0
NOVELTY_UNIT = 8192.0
LOG_UNIT = 256.0
LOW_UNIT = 16384.0
TILE = 256
VMEM_BYTES = 24 * 2**20


def dot(a, b, contract):
    return lax.dot_general(a, b, ((contract[:1], contract[1:]), ((), ())), preferred_element_type=jnp.float32)


def slot_of(cluster, rank, clusters):
    return rank // 2 * (2 * clusters) + cluster * 2 + rank % 2


def shifted(value, count):
    return jnp.concatenate([value[:, -count:], value[:, :-count]], axis=1) if count else value


def cluster_pairs(cluster_ref):
    across = jnp.broadcast_to(cluster_ref[...], (cluster_ref.shape[1],) * 2)
    down = across.T
    i = lax.broadcasted_iota(jnp.int32, across.shape, 0)
    j = lax.broadcasted_iota(jnp.int32, across.shape, 1)
    return across, down, i, j


def place_kernel(cluster_hbm, queries_hbm, out_ref, cluster_ref, queries_ref, cluster_sem, queries_sem):
    copy_cluster = pltpu.make_async_copy(cluster_hbm, cluster_ref, cluster_sem)
    copy_queries = pltpu.make_async_copy(queries_hbm, queries_ref, queries_sem)
    copy_cluster.start()
    copy_queries.start()
    copy_cluster.wait()
    across, down, i, j = cluster_pairs(cluster_ref)
    rows, features = queries_ref.shape
    clusters, pair, _ = out_ref.shape
    rank = jnp.sum(jnp.where((across == down) & (i < j), 1.0, 0.0), axis=0, keepdims=True)
    slot = slot_of(across[:1], rank.astype(jnp.int32), clusters)
    step = clusters * pair
    place = jnp.where(lax.broadcasted_iota(jnp.int32, (SIDE * step, rows), 0) == slot, 1.0, 0.0)
    place = place.astype(jnp.bfloat16)
    extra = jnp.zeros((step, EXTRA), jnp.float32)
    for h in range(SIDE):
        at = h * (EXTRA // SIDE)
        tail = jnp.where(j == at, i.astype(jnp.float32), jnp.where(j == at + 1, 1.0, 0.0))
        extra = extra + dot(place[h * step : (h + 1) * step], tail.astype(jnp.bfloat16), (1, 0))
    out_ref[:, :, SIDE * features :] = extra.astype(jnp.bfloat16).reshape(clusters, pair, EXTRA)
    copy_queries.wait()
    for h in range(SIDE):
        sent = dot(place[h * step : (h + 1) * step], queries_ref[...], (1, 0)).astype(jnp.bfloat16)
        out_ref[:, :, h * features : (h + 1) * features] = sent.reshape(clusters, pair, features)


def scale_kernel(store_hbm, scale_ref, near_ref, rest_ref, near_sem, rest_sem):
    near = near_ref.shape[0]
    copies = [
        pltpu.make_async_copy(store_hbm.at[pl.ds(0, near)], near_ref, near_sem),
        pltpu.make_async_copy(store_hbm.at[pl.ds(near, rest_ref.shape[0])], rest_ref, rest_sem),
    ]
    for copy in copies:
        copy.start()
    for copy, held, base in zip(copies, (near_ref, rest_ref), (0, near)):
        copy.wait()
        for at in range(0, held.shape[0], 128):
            wide = held[at : at + 128, :].astype(jnp.float32)
            wide = wide * wide
            total = wide[:, :128]
            for k in range(128, wide.shape[1], 128):
                total = total + wide[:, k : k + 128]
            total = jnp.sum(total.T, axis=0, keepdims=True)
            scale_ref[:, base + at : base + at + 128] = lax.rsqrt(total + epsilon)


def parts(value, unit):
    high = jnp.round(value * unit)
    return [high, jnp.round((value * unit - high) * LOW_UNIT)]


def cosines(rows, row_scale, held_ref, scale_ref, live, base, one, two, cos_ref):
    lane = lax.broadcasted_iota(jnp.int32, one.shape, 1)
    for t in range(0, held_ref.shape[0], TILE):
        raw = dot(rows, held_ref[t : t + TILE, :], (1, 1))
        for h in range(0, TILE, 128):
            at = t + h
            cosine = raw[:, h : h + 128] * row_scale * scale_ref[:, base + at : base + at + 128]
            cosine = jnp.where(lane < live - base - at, cosine, -2.0)
            cos_ref[:, at : at + 128] = cosine
            two = jnp.maximum(two, jnp.minimum(one, cosine))
            one = jnp.maximum(one, cosine)
    return one, two


def near_kernel(info_ref, got_ref, near_ref, scale_ref, cos_ref, rows_ref, state_ref):
    sources, pair, width = got_ref.shape
    features = (width - EXTRA) // SIDE
    step = sources * pair
    slots = SIDE * step
    extra = got_ref[:, :, SIDE * features :].reshape(step, EXTRA).astype(jnp.float32)
    for h in range(SIDE):
        span = slice(h * step, (h + 1) * step)
        rows_ref[span, :features] = got_ref[:, :, h * features : (h + 1) * features].reshape(step, features)
        rows_ref[span, features:] = shifted(extra, h * (EXTRA // SIDE)).astype(rows_ref.dtype)
    rows = rows_ref[:, :features]
    wide = rows.astype(jnp.float32)
    row_scale = lax.rsqrt(jnp.sum(wide * wide, axis=1, keepdims=True) + epsilon)
    state_ref[0] = jnp.broadcast_to(row_scale, (slots, 128))
    one = jnp.full((slots, 128), -3.0, jnp.float32)
    state_ref[1], state_ref[2] = cosines(rows, row_scale, near_ref, scale_ref, info_ref[0], 0, one, one, cos_ref)


def rest_kernel(
    growth, n_batch, rows_dev, n_store, info_ref, rows_ref, state_ref, rest_ref, scale_ref, cos_ref, best_ref, sums_ref
):
    slots, width = rows_ref.shape
    features = width - EXTRA
    live, batch = info_ref[0], info_ref[1]
    tail = rows_ref[:, features:].astype(jnp.float32)
    slot = lax.broadcasted_iota(jnp.int32, (slots, 1), 0)
    index = (slot % (2 * n_store) // 2 * n_batch + batch) * rows_dev + tail[:, :1].astype(jnp.int32)
    recency = jnp.exp(index.astype(jnp.float32) * growth) * tail[:, 1:2]
    base = scale_ref.shape[1] - rest_ref.shape[0]
    one, two = cosines(
        rows_ref[:, :features], state_ref[0][:, :1], rest_ref, scale_ref, live, base, state_ref[1], state_ref[2], cos_ref
    )
    lane = lax.broadcasted_iota(jnp.int32, (slots, 128), 1)
    first = jnp.max(one, axis=1, keepdims=True)
    holder = jnp.min(jnp.where(one == first, lane, 128), axis=1, keepdims=True)
    second = jnp.max(jnp.where(lane == holder, two, one), axis=1, keepdims=True)
    best_ref[...] = jnp.where(lane == 0, first, second)
    across = lax.broadcasted_iota(jnp.int32, sums_ref.shape, 1)
    sums_ref[...] = jnp.where(
        across == 0,
        jnp.sum(recency * first, axis=0, keepdims=True),
        jnp.sum(recency, axis=0, keepdims=True),
    )


def weigh_kernel(info_ref, cos_near_ref, cos_rest_ref, best_ref, near_ref, rest_ref, weighted_ref, total_ref, expo_ref):
    slots, near = cos_near_ref.shape
    live = info_ref[0]
    first = best_ref[:, :1]
    lane = lax.broadcasted_iota(jnp.int32, (slots, 128), 1)
    total = jnp.zeros((slots, 128), jnp.float32)
    for cos_ref, base in ((cos_near_ref, 0), (cos_rest_ref, near)):
        for at in range(0, cos_ref.shape[1], 128):
            expo = jnp.exp(normalized_sharpness * (cos_ref[:, at : at + 128] - first))
            expo = jnp.where(lane < live - base - at, expo, 0.0)
            total = total + expo
            expo_ref[:, base + at : base + at + 128] = expo.astype(jnp.bfloat16)
    total_ref[...] = total
    weighted = dot(expo_ref[:, :near], near_ref[...], (1, 0))
    weighted_ref[...] = weighted + dot(expo_ref[:, near:], rest_ref[...], (1, 0))


def code_kernel(weighted_ref, total_ref, best_ref, *refs):
    *sums_refs, out_ref = refs
    sources, pair, width = out_ref.shape
    features = (width - EXTRA) // SIDE
    step = sources * pair
    slots = SIDE * step
    sums = sums_refs[0][...]
    for ref in sums_refs[1:]:
        sums = sums + ref[...]
    mean = sums[:, :1] / sums[:, 1:2]
    first, second = best_ref[:, :1], best_ref[:, 1:2]
    total = jnp.sum(total_ref[...], axis=1, keepdims=True)
    weighted = weighted_ref[...]
    largest = jnp.maximum(jnp.max(jnp.abs(weighted), axis=1, keepdims=True), 1e-30)
    coded = jnp.round(weighted * (STEPS / largest)).astype(jnp.int32).astype(jnp.int16)
    for h in range(SIDE):
        part = coded[h * step : (h + 1) * step].reshape(sources, pair, features)
        out_ref[:, :, h * features : (h + 1) * features] = part
    values = (
        parts(first, COSINE_UNIT)
        + parts(second, COSINE_UNIT)
        + parts(jnp.log(largest / total), LOG_UNIT)
        + parts(first - mean, NOVELTY_UNIT)
    )
    lane = lax.broadcasted_iota(jnp.int32, (step, EXTRA), 1)
    extra = jnp.zeros((step, EXTRA), jnp.float32)
    for k, value in enumerate(values):
        for h in range(SIDE):
            extra = jnp.where(lane == k + h * (EXTRA // SIDE), value[h * step : (h + 1) * step], extra)
    extra = extra.astype(jnp.int32).astype(jnp.int16)
    out_ref[:, :, SIDE * features :] = extra.reshape(sources, pair, EXTRA)


def joined(high, low, unit):
    return (high + low * (1.0 / LOW_UNIT)) * (1.0 / unit)


def pick_kernel(cluster_ref, back_ref, near_ref, best_ref, novelty_ref):
    across, down, i, j = cluster_pairs(cluster_ref)
    clusters, pair, width = back_ref.shape
    features = (width - EXTRA) // SIDE
    step = clusters * pair
    rank = jnp.sum(jnp.where((across == down) & (j < i), 1.0, 0.0), axis=1, keepdims=True)
    slot = slot_of(down[:, :1], rank.astype(jnp.int32), clusters)
    pick = jnp.where(lax.broadcasted_iota(jnp.int32, (i.shape[0], SIDE * step), 1) == slot, 1.0, 0.0)
    pick = pick.astype(jnp.bfloat16)

    pick = jnp.concatenate([pick, pick], axis=1)

    def mine(halves):
        value = jnp.concatenate(halves, axis=0).astype(jnp.float32)
        high = jnp.floor(value * (1.0 / 256.0)) * 256.0
        return dot(pick, jnp.concatenate([high, value - high], axis=0).astype(jnp.bfloat16), (1, 0))

    extra = back_ref[:, :, SIDE * features :].reshape(step, EXTRA).astype(jnp.float32)
    extra = mine([shifted(extra, h * (EXTRA // SIDE)) for h in range(SIDE)])
    largest = jnp.exp(joined(extra[:, 4:5], extra[:, 5:6], LOG_UNIT))
    rows = mine([back_ref[:, :, h * features : (h + 1) * features].reshape(step, features) for h in range(SIDE)])
    near_ref[...] = rows * (largest * (1.0 / STEPS))
    extra = extra.T
    best_ref[0:1, :] = joined(extra[0:1], extra[1:2], COSINE_UNIT)
    best_ref[1:2, :] = joined(extra[2:3], extra[3:4], COSINE_UNIT)
    novelty_ref[...] = joined(extra[6:7], extra[7:8], NOVELTY_UNIT)


def over_batch(value):
    n = lax.axis_size("batch")
    shifts = sorted(range(1, n), key=lambda k: -min(k, n - k))
    return [value] + [lax.ppermute(value, "batch", [(i, (i + k) % n) for i in range(n)]) for k in shifts]


def body(queries, query_cluster, store, store_counts):
    n_store = lax.axis_size("store")
    n_batch = lax.axis_size("batch")
    rows_dev, features = queries.shape
    clusters = store_counts.shape[0]
    crows = store.shape[0]
    depth = 2 * rows_dev // clusters
    slots = clusters * depth
    pair = depth // SIDE
    width = features + EXTRA
    wide = SIDE * features + EXTRA
    growth = math.log(3.0) / (rows_dev * n_store * n_batch)
    params = pltpu.CompilerParams(vmem_limit_bytes=VMEM_BYTES)

    cluster_row = query_cluster.reshape(1, rows_dev)
    send = pl.pallas_call(
        place_kernel,
        out_shape=jax.ShapeDtypeStruct((clusters, pair, wide), jnp.bfloat16),
        in_specs=[pl.BlockSpec(memory_space=pltpu.HBM)] * 2,
        scratch_shapes=[
            pltpu.VMEM((1, rows_dev), jnp.int32),
            pltpu.VMEM((rows_dev, features), jnp.bfloat16),
            pltpu.SemaphoreType.DMA,
            pltpu.SemaphoreType.DMA,
        ],
        compiler_params=pltpu.CompilerParams(vmem_limit_bytes=60 * 2**20),
    )(cluster_row, queries)

    info = jnp.stack([store_counts[lax.axis_index("store")], lax.axis_index("batch")])
    near = crows // 2
    f32, bf16 = jnp.float32, store.dtype
    vmem = pl.BlockSpec(memory_space=pltpu.VMEM)
    hbm = pl.BlockSpec(memory_space=pltpu.HBM)
    smem = pl.BlockSpec(memory_space=pltpu.SMEM)
    store_scale, store_near, store_rest = pl.pallas_call(
        scale_kernel,
        out_shape=(
            jax.ShapeDtypeStruct((1, crows), f32),
            jax.ShapeDtypeStruct((near, features), bf16),
            jax.ShapeDtypeStruct((crows - near, features), bf16),
        ),
        in_specs=[hbm],
        out_specs=(vmem,) * 3,
        scratch_shapes=[pltpu.SemaphoreType.DMA, pltpu.SemaphoreType.DMA],
        compiler_params=params,
        cost_estimate=pl.CostEstimate(flops=2 * crows * features, bytes_accessed=2 * crows * features, transcendentals=crows),
    )(store)
    got = lax.all_to_all(send, "store", split_axis=0, concat_axis=0, tiled=True)

    half_cost = pl.CostEstimate(flops=slots * crows * features, bytes_accessed=crows * features, transcendentals=0)
    cos_near, rows, state = pl.pallas_call(
        near_kernel,
        out_shape=(
            jax.ShapeDtypeStruct((slots, near), f32),
            jax.ShapeDtypeStruct((slots, width), bf16),
            jax.ShapeDtypeStruct((3, slots, 128), f32),
        ),
        in_specs=[smem, vmem, vmem, vmem],
        out_specs=(vmem,) * 3,
        compiler_params=params,
        cost_estimate=half_cost,
    )(info, got, store_near, store_scale)
    cos_rest, best, sums = pl.pallas_call(
        functools.partial(rest_kernel, growth, n_batch, rows_dev, n_store),
        out_shape=(
            jax.ShapeDtypeStruct((slots, crows - near), f32),
            jax.ShapeDtypeStruct((slots, 128), f32),
            jax.ShapeDtypeStruct((1, 128), f32),
        ),
        in_specs=[smem, vmem, vmem, vmem, vmem],
        out_specs=(vmem,) * 3,
        compiler_params=params,
        cost_estimate=half_cost,
    )(info, rows, state, store_rest, store_scale)
    sums = over_batch(sums)
    weighted, total = pl.pallas_call(
        weigh_kernel,
        out_shape=(
            jax.ShapeDtypeStruct((slots, features), jnp.float32),
            jax.ShapeDtypeStruct((slots, 128), jnp.float32),
        ),
        in_specs=[smem] + [vmem] * 5,
        out_specs=(vmem, vmem),
        scratch_shapes=[pltpu.VMEM((slots, crows), jnp.bfloat16)],
        compiler_params=params,
        cost_estimate=pl.CostEstimate(flops=4 * slots * crows * features, bytes_accessed=8 * crows * features, transcendentals=slots * crows),
    )(info, cos_near, cos_rest, best, store_near, store_rest)
    back = pl.pallas_call(
        code_kernel,
        out_shape=jax.ShapeDtypeStruct((n_store, pair, wide), jnp.int16),
        in_specs=[vmem] * (3 + n_batch),
        out_specs=vmem,
        compiler_params=params,
    )(weighted, total, best, *sums)
    back = lax.all_to_all(back, "store", split_axis=0, concat_axis=0, tiled=True)

    neighbours, best, novelty = pl.pallas_call(
        pick_kernel,
        out_shape=(
            jax.ShapeDtypeStruct((rows_dev, features), jnp.float32),
            jax.ShapeDtypeStruct((2, rows_dev), jnp.float32),
            jax.ShapeDtypeStruct((1, rows_dev), jnp.float32),
        ),
        compiler_params=params,
    )(cluster_row, back)
    return (best.T, novelty[0], neighbours)


def solution(mesh):
    in_specs = (P(("store", "batch"), None), P(("store", "batch")), P("store", None), P())
    out_specs = (P(("store", "batch"), None), P(("store", "batch")), P(("store", "batch"), None))
    return jax.shard_map(body, mesh=mesh, in_specs=in_specs, out_specs=out_specs, check_vma=False)
```

```python
import functools
import math

import jax
import jax.numpy as jnp
from jax import lax
from jax.experimental import pallas as pl
from jax.experimental.pallas import tpu as pltpu
from jax.sharding import PartitionSpec as P

normalized_sharpness = 160.0
epsilon = 1e-06
EXTRA = 128
SIDE = 2
STEPS = 32767.0
COSINE_UNIT = 16384.0
NOVELTY_UNIT = 8192.0
LOG_UNIT = 256.0
LOW_UNIT = 16384.0
TILE = 256
VMEM_BYTES = 24 * 2**20


def dot(a, b, contract):
    return lax.dot_general(a, b, ((contract[:1], contract[1:]), ((), ())), preferred_element_type=jnp.float32)


def slot_of(cluster, rank, clusters):
    return rank // 2 * (2 * clusters) + cluster * 2 + rank % 2


def shifted(value, count):
    return jnp.concatenate([value[:, -count:], value[:, :-count]], axis=1) if count else value


def cluster_pairs(cluster_ref):
    across = jnp.broadcast_to(cluster_ref[...], (cluster_ref.shape[1],) * 2)
    down = across.T
    i = lax.broadcasted_iota(jnp.int32, across.shape, 0)
    j = lax.broadcasted_iota(jnp.int32, across.shape, 1)
    return across, down, i, j


def place_kernel(cluster_hbm, queries_hbm, out_ref, cluster_ref, queries_ref, cluster_sem, queries_sem):
    copy_cluster = pltpu.make_async_copy(cluster_hbm, cluster_ref, cluster_sem)
    copy_queries = pltpu.make_async_copy(queries_hbm, queries_ref, queries_sem)
    copy_cluster.start()
    copy_queries.start()
    copy_cluster.wait()
    across, down, i, j = cluster_pairs(cluster_ref)
    rows, features = queries_ref.shape
    clusters, pair, _ = out_ref.shape
    rank = jnp.sum(jnp.where((across == down) & (i < j), 1.0, 0.0), axis=0, keepdims=True)
    slot = slot_of(across[:1], rank.astype(jnp.int32), clusters)
    step = clusters * pair
    place = jnp.where(lax.broadcasted_iota(jnp.int32, (SIDE * step, rows), 0) == slot, 1.0, 0.0)
    place = place.astype(jnp.bfloat16)
    extra = jnp.zeros((step, EXTRA), jnp.float32)
    for h in range(SIDE):
        at = h * (EXTRA // SIDE)
        tail = jnp.where(j == at, i.astype(jnp.float32), jnp.where(j == at + 1, 1.0, 0.0))
        extra = extra + dot(place[h * step : (h + 1) * step], tail.astype(jnp.bfloat16), (1, 0))
    out_ref[:, :, SIDE * features :] = extra.astype(jnp.bfloat16).reshape(clusters, pair, EXTRA)
    copy_queries.wait()
    for h in range(SIDE):
        sent = dot(place[h * step : (h + 1) * step], queries_ref[...], (1, 0)).astype(jnp.bfloat16)
        out_ref[:, :, h * features : (h + 1) * features] = sent.reshape(clusters, pair, features)


def scale_kernel(store_hbm, scale_ref, near_ref, rest_ref, near_sem, rest_sem):
    near = near_ref.shape[0]
    copies = [
        pltpu.make_async_copy(store_hbm.at[pl.ds(0, near)], near_ref, near_sem),
        pltpu.make_async_copy(store_hbm.at[pl.ds(near, rest_ref.shape[0])], rest_ref, rest_sem),
    ]
    for copy in copies:
        copy.start()
    for copy, held, base in zip(copies, (near_ref, rest_ref), (0, near)):
        copy.wait()
        for at in range(0, held.shape[0], 128):
            wide = held[at : at + 128, :].astype(jnp.float32)
            wide = wide * wide
            total = wide[:, :128]
            for k in range(128, wide.shape[1], 128):
                total = total + wide[:, k : k + 128]
            total = jnp.sum(total.T, axis=0, keepdims=True)
            scale_ref[:, base + at : base + at + 128] = lax.rsqrt(total + epsilon)


def parts(value, unit):
    high = jnp.round(value * unit)
    return [high, jnp.round((value * unit - high) * LOW_UNIT)]


def cosines(rows, row_scale, held_ref, scale_ref, live, base, one, two, cos_ref):
    lane = lax.broadcasted_iota(jnp.int32, one.shape, 1)
    for t in range(0, held_ref.shape[0], TILE):
        raw = dot(rows, held_ref[t : t + TILE, :], (1, 1))
        for h in range(0, TILE, 128):
            at = t + h
            cosine = raw[:, h : h + 128] * row_scale * scale_ref[:, base + at : base + at + 128]
            cosine = jnp.where(lane < live - base - at, cosine, -2.0)
            cos_ref[:, at : at + 128] = cosine
            two = jnp.maximum(two, jnp.minimum(one, cosine))
            one = jnp.maximum(one, cosine)
    return one, two


def near_kernel(info_ref, got_ref, near_ref, scale_ref, cos_ref, rows_ref, state_ref):
    sources, pair, width = got_ref.shape
    features = (width - EXTRA) // SIDE
    step = sources * pair
    slots = SIDE * step
    extra = got_ref[:, :, SIDE * features :].reshape(step, EXTRA).astype(jnp.float32)
    for h in range(SIDE):
        span = slice(h * step, (h + 1) * step)
        rows_ref[span, :features] = got_ref[:, :, h * features : (h + 1) * features].reshape(step, features)
        rows_ref[span, features:] = shifted(extra, h * (EXTRA // SIDE)).astype(rows_ref.dtype)
    rows = rows_ref[:, :features]
    wide = rows.astype(jnp.float32)
    row_scale = lax.rsqrt(jnp.sum(wide * wide, axis=1, keepdims=True) + epsilon)
    state_ref[0] = jnp.broadcast_to(row_scale, (slots, 128))
    one = jnp.full((slots, 128), -3.0, jnp.float32)
    state_ref[1], state_ref[2] = cosines(rows, row_scale, near_ref, scale_ref, info_ref[0], 0, one, one, cos_ref)


def rest_kernel(
    growth, n_batch, rows_dev, n_store, info_ref, rows_ref, state_ref, rest_ref, scale_ref, cos_ref, best_ref, sums_ref
):
    slots, width = rows_ref.shape
    features = width - EXTRA
    live, batch = info_ref[0], info_ref[1]
    tail = rows_ref[:, features:].astype(jnp.float32)
    slot = lax.broadcasted_iota(jnp.int32, (slots, 1), 0)
    index = (slot % (2 * n_store) // 2 * n_batch + batch) * rows_dev + tail[:, :1].astype(jnp.int32)
    recency = jnp.exp(index.astype(jnp.float32) * growth) * tail[:, 1:2]
    base = scale_ref.shape[1] - rest_ref.shape[0]
    one, two = cosines(
        rows_ref[:, :features], state_ref[0][:, :1], rest_ref, scale_ref, live, base, state_ref[1], state_ref[2], cos_ref
    )
    lane = lax.broadcasted_iota(jnp.int32, (slots, 128), 1)
    first = jnp.max(one, axis=1, keepdims=True)
    holder = jnp.min(jnp.where(one == first, lane, 128), axis=1, keepdims=True)
    second = jnp.max(jnp.where(lane == holder, two, one), axis=1, keepdims=True)
    best_ref[...] = jnp.where(lane == 0, first, second)
    across = lax.broadcasted_iota(jnp.int32, sums_ref.shape, 1)
    sums_ref[...] = jnp.where(
        across == 0,
        jnp.sum(recency * first, axis=0, keepdims=True),
        jnp.sum(recency, axis=0, keepdims=True),
    )


def weigh_kernel(info_ref, cos_near_ref, cos_rest_ref, best_ref, near_ref, rest_ref, weighted_ref, total_ref, expo_ref):
    slots, near = cos_near_ref.shape
    live = info_ref[0]
    first = best_ref[:, :1]
    lane = lax.broadcasted_iota(jnp.int32, (slots, 128), 1)
    total = jnp.zeros((slots, 128), jnp.float32)
    for cos_ref, base in ((cos_near_ref, 0), (cos_rest_ref, near)):
        for at in range(0, cos_ref.shape[1], 128):
            expo = jnp.exp(normalized_sharpness * (cos_ref[:, at : at + 128] - first))
            expo = jnp.where(lane < live - base - at, expo, 0.0)
            total = total + expo
            expo_ref[:, base + at : base + at + 128] = expo.astype(jnp.bfloat16)
    total_ref[...] = total
    weighted = dot(expo_ref[:, :near], near_ref[...], (1, 0))
    weighted_ref[...] = weighted + dot(expo_ref[:, near:], rest_ref[...], (1, 0))


def code_kernel(weighted_ref, total_ref, best_ref, *refs):
    *sums_refs, out_ref = refs
    sources, pair, width = out_ref.shape
    features = (width - EXTRA) // SIDE
    step = sources * pair
    slots = SIDE * step
    sums = sums_refs[0][...]
    for ref in sums_refs[1:]:
        sums = sums + ref[...]
    mean = sums[:, :1] / sums[:, 1:2]
    first, second = best_ref[:, :1], best_ref[:, 1:2]
    total = jnp.sum(total_ref[...], axis=1, keepdims=True)
    weighted = weighted_ref[...]
    largest = jnp.maximum(jnp.max(jnp.abs(weighted), axis=1, keepdims=True), 1e-30)
    coded = jnp.round(weighted * (STEPS / largest)).astype(jnp.int32).astype(jnp.int16)
    for h in range(SIDE):
        part = coded[h * step : (h + 1) * step].reshape(sources, pair, features)
        out_ref[:, :, h * features : (h + 1) * features] = part
    values = (
        parts(first, COSINE_UNIT)
        + parts(second, COSINE_UNIT)
        + parts(jnp.log(largest / total), LOG_UNIT)
        + parts(first - mean, NOVELTY_UNIT)
    )
    lane = lax.broadcasted_iota(jnp.int32, (step, EXTRA), 1)
    extra = jnp.zeros((step, EXTRA), jnp.float32)
    for k, value in enumerate(values):
        for h in range(SIDE):
            extra = jnp.where(lane == k + h * (EXTRA // SIDE), value[h * step : (h + 1) * step], extra)
    extra = extra.astype(jnp.int32).astype(jnp.int16)
    out_ref[:, :, SIDE * features :] = extra.reshape(sources, pair, EXTRA)


def joined(high, low, unit):
    return (high + low * (1.0 / LOW_UNIT)) * (1.0 / unit)


def pick_kernel(cluster_ref, back_ref, near_hbm, best_ref, novelty_ref, near_ref, sems):
    across, down, i, j = cluster_pairs(cluster_ref)
    clusters, pair, width = back_ref.shape
    features = (width - EXTRA) // SIDE
    step = clusters * pair
    rank = jnp.sum(jnp.where((across == down) & (j < i), 1.0, 0.0), axis=1, keepdims=True)
    slot = slot_of(down[:, :1], rank.astype(jnp.int32), clusters)
    pick = jnp.where(lax.broadcasted_iota(jnp.int32, (i.shape[0], SIDE * step), 1) == slot, 1.0, 0.0)
    pick = pick.astype(jnp.bfloat16)

    pick = jnp.concatenate([pick, pick], axis=1)

    def terms(halves):
        value = jnp.concatenate(halves, axis=0).astype(jnp.float32)
        high = jnp.floor(value * (1.0 / 256.0)) * 256.0
        return jnp.concatenate([high, value - high], axis=0).astype(jnp.bfloat16)

    extra = back_ref[:, :, SIDE * features :].reshape(step, EXTRA).astype(jnp.float32)
    extra = dot(pick, terms([shifted(extra, h * (EXTRA // SIDE)) for h in range(SIDE)]), (1, 0))
    largest = jnp.exp(joined(extra[:, 4:5], extra[:, 5:6], LOG_UNIT))
    rows = terms([back_ref[:, :, h * features : (h + 1) * features].reshape(step, features) for h in range(SIDE)])
    factor = largest * (1.0 / STEPS)
    count = near_ref.shape[0] // sems.shape[0]
    copies = []
    for p in range(sems.shape[0]):
        at = p * count
        near_ref[at : at + count, :] = dot(pick[at : at + count], rows, (1, 0)) * factor[at : at + count]
        span = pl.ds(at, count)
        copies.append(pltpu.make_async_copy(near_ref.at[span], near_hbm.at[span], sems.at[p]))
        copies[-1].start()
    extra = extra.T
    best_ref[0:1, :] = joined(extra[0:1], extra[1:2], COSINE_UNIT)
    best_ref[1:2, :] = joined(extra[2:3], extra[3:4], COSINE_UNIT)
    novelty_ref[...] = joined(extra[6:7], extra[7:8], NOVELTY_UNIT)
    for copy in copies:
        copy.wait()


def over_batch(value):
    n = lax.axis_size("batch")
    shifts = sorted(range(1, n), key=lambda k: -min(k, n - k))
    return [value] + [lax.ppermute(value, "batch", [(i, (i + k) % n) for i in range(n)]) for k in shifts]


def body(queries, query_cluster, store, store_counts):
    n_store = lax.axis_size("store")
    n_batch = lax.axis_size("batch")
    rows_dev, features = queries.shape
    clusters = store_counts.shape[0]
    crows = store.shape[0]
    depth = 2 * rows_dev // clusters
    slots = clusters * depth
    pair = depth // SIDE
    width = features + EXTRA
    wide = SIDE * features + EXTRA
    growth = math.log(3.0) / (rows_dev * n_store * n_batch)
    params = pltpu.CompilerParams(vmem_limit_bytes=VMEM_BYTES)

    cluster_row = query_cluster.reshape(1, rows_dev)
    send = pl.pallas_call(
        place_kernel,
        out_shape=jax.ShapeDtypeStruct((clusters, pair, wide), jnp.bfloat16),
        in_specs=[pl.BlockSpec(memory_space=pltpu.HBM)] * 2,
        scratch_shapes=[
            pltpu.VMEM((1, rows_dev), jnp.int32),
            pltpu.VMEM((rows_dev, features), jnp.bfloat16),
            pltpu.SemaphoreType.DMA,
            pltpu.SemaphoreType.DMA,
        ],
        compiler_params=pltpu.CompilerParams(vmem_limit_bytes=60 * 2**20),
    )(cluster_row, queries)

    info = jnp.stack([store_counts[lax.axis_index("store")], lax.axis_index("batch")])
    near = crows // 2
    f32, bf16 = jnp.float32, store.dtype
    vmem = pl.BlockSpec(memory_space=pltpu.VMEM)
    hbm = pl.BlockSpec(memory_space=pltpu.HBM)
    smem = pl.BlockSpec(memory_space=pltpu.SMEM)
    store_scale, store_near, store_rest = pl.pallas_call(
        scale_kernel,
        out_shape=(
            jax.ShapeDtypeStruct((1, crows), f32),
            jax.ShapeDtypeStruct((near, features), bf16),
            jax.ShapeDtypeStruct((crows - near, features), bf16),
        ),
        in_specs=[hbm],
        out_specs=(vmem,) * 3,
        scratch_shapes=[pltpu.SemaphoreType.DMA, pltpu.SemaphoreType.DMA],
        compiler_params=params,
        cost_estimate=pl.CostEstimate(flops=2 * crows * features, bytes_accessed=2 * crows * features, transcendentals=crows),
    )(store)
    got = lax.all_to_all(send, "store", split_axis=0, concat_axis=0, tiled=True)

    half_cost = pl.CostEstimate(flops=slots * crows * features, bytes_accessed=crows * features, transcendentals=0)
    cos_near, rows, state = pl.pallas_call(
        near_kernel,
        out_shape=(
            jax.ShapeDtypeStruct((slots, near), f32),
            jax.ShapeDtypeStruct((slots, width), bf16),
            jax.ShapeDtypeStruct((3, slots, 128), f32),
        ),
        in_specs=[smem, vmem, vmem, vmem],
        out_specs=(vmem,) * 3,
        compiler_params=params,
        cost_estimate=half_cost,
    )(info, got, store_near, store_scale)
    cos_rest, best, sums = pl.pallas_call(
        functools.partial(rest_kernel, growth, n_batch, rows_dev, n_store),
        out_shape=(
            jax.ShapeDtypeStruct((slots, crows - near), f32),
            jax.ShapeDtypeStruct((slots, 128), f32),
            jax.ShapeDtypeStruct((1, 128), f32),
        ),
        in_specs=[smem, vmem, vmem, vmem, vmem],
        out_specs=(vmem,) * 3,
        compiler_params=params,
        cost_estimate=half_cost,
    )(info, rows, state, store_rest, store_scale)
    sums = over_batch(sums)
    weighted, total = pl.pallas_call(
        weigh_kernel,
        out_shape=(
            jax.ShapeDtypeStruct((slots, features), jnp.float32),
            jax.ShapeDtypeStruct((slots, 128), jnp.float32),
        ),
        in_specs=[smem] + [vmem] * 5,
        out_specs=(vmem, vmem),
        scratch_shapes=[pltpu.VMEM((slots, crows), jnp.bfloat16)],
        compiler_params=params,
        cost_estimate=pl.CostEstimate(flops=4 * slots * crows * features, bytes_accessed=8 * crows * features, transcendentals=slots * crows),
    )(info, cos_near, cos_rest, best, store_near, store_rest)
    back = pl.pallas_call(
        code_kernel,
        out_shape=jax.ShapeDtypeStruct((n_store, pair, wide), jnp.int16),
        in_specs=[vmem] * (3 + n_batch),
        out_specs=vmem,
        compiler_params=params,
    )(weighted, total, best, *sums)
    back = lax.all_to_all(back, "store", split_axis=0, concat_axis=0, tiled=True)

    neighbours, best, novelty = pl.pallas_call(
        pick_kernel,
        out_shape=(
            jax.ShapeDtypeStruct((rows_dev, features), jnp.float32),
            jax.ShapeDtypeStruct((2, rows_dev), jnp.float32),
            jax.ShapeDtypeStruct((1, rows_dev), jnp.float32),
        ),
        in_specs=[vmem, vmem],
        out_specs=(hbm, vmem, vmem),
        scratch_shapes=[pltpu.VMEM((rows_dev, features), f32), pltpu.SemaphoreType.DMA((2,))],
        compiler_params=params,
    )(cluster_row, back)
    return (best.T, novelty[0], neighbours)


def solution(mesh):
    in_specs = (P(("store", "batch"), None), P(("store", "batch")), P("store", None), P())
    out_specs = (P(("store", "batch"), None), P(("store", "batch")), P(("store", "batch"), None))
    return jax.shard_map(body, mesh=mesh, in_specs=in_specs, out_specs=out_specs, check_vma=False)
```

```python
import functools
import math

import jax
import jax.numpy as jnp
from jax import lax
from jax.experimental import pallas as pl
from jax.experimental.pallas import tpu as pltpu
from jax.sharding import PartitionSpec as P

normalized_sharpness = 160.0
epsilon = 1e-06
EXTRA = 128
SIDE = 2
STEPS = 32767.0
NOT_LIVE = -1e30
COSINE_UNIT = 16384.0
NOVELTY_UNIT = 8192.0
LOG_UNIT = 256.0
LOW_UNIT = 16384.0
TILE = 256
VMEM_BYTES = 24 * 2**20


def dot(a, b, contract):
    return lax.dot_general(a, b, ((contract[:1], contract[1:]), ((), ())), preferred_element_type=jnp.float32)


def slot_of(cluster, rank, clusters):
    return rank // 2 * (2 * clusters) + cluster * 2 + rank % 2


def shifted(value, count):
    return jnp.concatenate([value[:, -count:], value[:, :-count]], axis=1) if count else value


def cluster_pairs(cluster_ref):
    across = jnp.broadcast_to(cluster_ref[...], (cluster_ref.shape[1],) * 2)
    down = across.T
    i = lax.broadcasted_iota(jnp.int32, across.shape, 0)
    j = lax.broadcasted_iota(jnp.int32, across.shape, 1)
    return across, down, i, j


def place_kernel(cluster_hbm, queries_hbm, out_ref, cluster_ref, queries_ref, cluster_sem, queries_sem):
    copy_cluster = pltpu.make_async_copy(cluster_hbm, cluster_ref, cluster_sem)
    copy_queries = pltpu.make_async_copy(queries_hbm, queries_ref, queries_sem)
    copy_cluster.start()
    copy_queries.start()
    copy_cluster.wait()
    across, down, i, j = cluster_pairs(cluster_ref)
    rows, features = queries_ref.shape
    clusters, pair, _ = out_ref.shape
    rank = jnp.sum(jnp.where((across == down) & (i < j), 1.0, 0.0), axis=0, keepdims=True)
    slot = slot_of(across[:1], rank.astype(jnp.int32), clusters)
    step = clusters * pair
    place = jnp.where(lax.broadcasted_iota(jnp.int32, (SIDE * step, rows), 0) == slot, 1.0, 0.0)
    place = place.astype(jnp.bfloat16)
    extra = jnp.zeros((step, EXTRA), jnp.float32)
    for h in range(SIDE):
        at = h * (EXTRA // SIDE)
        tail = jnp.where(j == at, i.astype(jnp.float32), jnp.where(j == at + 1, 1.0, 0.0))
        extra = extra + dot(place[h * step : (h + 1) * step], tail.astype(jnp.bfloat16), (1, 0))
    out_ref[:, :, SIDE * features :] = extra.astype(jnp.bfloat16).reshape(clusters, pair, EXTRA)
    copy_queries.wait()
    for h in range(SIDE):
        sent = dot(place[h * step : (h + 1) * step], queries_ref[...], (1, 0)).astype(jnp.bfloat16)
        out_ref[:, :, h * features : (h + 1) * features] = sent.reshape(clusters, pair, features)


def scale_kernel(store_hbm, scale_ref, near_ref, rest_ref, near_sem, rest_sem):
    near = near_ref.shape[0]
    copies = [
        pltpu.make_async_copy(store_hbm.at[pl.ds(0, near)], near_ref, near_sem),
        pltpu.make_async_copy(store_hbm.at[pl.ds(near, rest_ref.shape[0])], rest_ref, rest_sem),
    ]
    for copy in copies:
        copy.start()
    for copy, held, base in zip(copies, (near_ref, rest_ref), (0, near)):
        copy.wait()
        for at in range(0, held.shape[0], 128):
            wide = held[at : at + 128, :].astype(jnp.float32)
            wide = wide * wide
            total = wide[:, :128]
            for k in range(128, wide.shape[1], 128):
                total = total + wide[:, k : k + 128]
            total = jnp.sum(total.T, axis=0, keepdims=True)
            scale_ref[:, base + at : base + at + 128] = lax.rsqrt(total + epsilon)


def parts(value, unit):
    high = jnp.round(value * unit)
    return [high, jnp.round((value * unit - high) * LOW_UNIT)]


def cosines(rows, held_ref, scale_ref, live, base, one, two, cos_ref):
    lane = lax.broadcasted_iota(jnp.int32, one.shape, 1)
    for t in range(0, held_ref.shape[0], TILE):
        raw = dot(rows, held_ref[t : t + TILE, :], (1, 1))
        for h in range(0, TILE, 128):
            at = t + h
            cosine = raw[:, h : h + 128] * scale_ref[:, base + at : base + at + 128]
            cosine = jnp.where(lane < live - base - at, cosine, NOT_LIVE)
            cos_ref[:, at : at + 128] = cosine
            two = jnp.maximum(two, jnp.minimum(one, cosine))
            one = jnp.maximum(one, cosine)
    return one, two


def near_kernel(info_ref, got_ref, near_ref, scale_ref, cos_ref, rows_ref, state_ref):
    sources, pair, width = got_ref.shape
    features = (width - EXTRA) // SIDE
    step = sources * pair
    slots = SIDE * step
    extra = got_ref[:, :, SIDE * features :].reshape(step, EXTRA).astype(jnp.float32)
    for h in range(SIDE):
        span = slice(h * step, (h + 1) * step)
        rows_ref[span, :features] = got_ref[:, :, h * features : (h + 1) * features].reshape(step, features)
        rows_ref[span, features:] = shifted(extra, h * (EXTRA // SIDE)).astype(rows_ref.dtype)
    one = jnp.full((slots, 128), 2.0 * NOT_LIVE, jnp.float32)
    state_ref[0], state_ref[1] = cosines(
        rows_ref[:, :features], near_ref, scale_ref, info_ref[0], 0, one, one, cos_ref
    )


def rest_kernel(
    growth, n_batch, rows_dev, n_store, info_ref, rows_ref, state_ref, rest_ref, scale_ref, cos_ref, best_ref, sums_ref
):
    slots, width = rows_ref.shape
    features = width - EXTRA
    live, batch = info_ref[0], info_ref[1]
    tail = rows_ref[:, features:].astype(jnp.float32)
    slot = lax.broadcasted_iota(jnp.int32, (slots, 1), 0)
    index = (slot % (2 * n_store) // 2 * n_batch + batch) * rows_dev + tail[:, :1].astype(jnp.int32)
    recency = jnp.exp(index.astype(jnp.float32) * growth) * tail[:, 1:2]
    base = scale_ref.shape[1] - rest_ref.shape[0]
    rows = rows_ref[:, :features]
    one, two = cosines(rows, rest_ref, scale_ref, live, base, state_ref[0], state_ref[1], cos_ref)
    wide = rows.astype(jnp.float32)
    row_scale = lax.rsqrt(jnp.sum(wide * wide, axis=1, keepdims=True) + epsilon)
    lane = lax.broadcasted_iota(jnp.int32, (slots, 128), 1)
    first = jnp.max(one, axis=1, keepdims=True)
    holder = jnp.min(jnp.where(one == first, lane, 128), axis=1, keepdims=True)
    second = jnp.max(jnp.where(lane == holder, two, one), axis=1, keepdims=True)
    best_ref[...] = jnp.where(
        lane == 0, first * row_scale, jnp.where(lane == 1, second * row_scale, jnp.where(lane == 2, first, row_scale))
    )
    first = first * row_scale
    across = lax.broadcasted_iota(jnp.int32, sums_ref.shape, 1)
    sums_ref[...] = jnp.where(
        across == 0,
        jnp.sum(recency * first, axis=0, keepdims=True),
        jnp.sum(recency, axis=0, keepdims=True),
    )


def weigh_kernel(info_ref, cos_near_ref, cos_rest_ref, best_ref, near_ref, rest_ref, weighted_ref, total_ref, expo_ref):
    slots, near = cos_near_ref.shape
    live = info_ref[0]
    first = best_ref[:, 2:3]
    factor = normalized_sharpness * best_ref[:, 3:4]
    lane = lax.broadcasted_iota(jnp.int32, (slots, 128), 1)
    total = jnp.zeros((slots, 128), jnp.float32)
    for cos_ref, base in ((cos_near_ref, 0), (cos_rest_ref, near)):
        for at in range(0, cos_ref.shape[1], 128):
            expo = jnp.exp(factor * (cos_ref[:, at : at + 128] - first))
            expo = jnp.where(lane < live - base - at, expo, 0.0)
            total = total + expo
            expo_ref[:, base + at : base + at + 128] = expo.astype(jnp.bfloat16)
    total_ref[...] = total
    weighted = dot(expo_ref[:, :near], near_ref[...], (1, 0))
    weighted_ref[...] = weighted + dot(expo_ref[:, near:], rest_ref[...], (1, 0))


def code_kernel(weighted_ref, total_ref, best_ref, *refs):
    *sums_refs, out_ref = refs
    sources, pair, width = out_ref.shape
    features = (width - EXTRA) // SIDE
    step = sources * pair
    slots = SIDE * step
    sums = sums_refs[0][...]
    for ref in sums_refs[1:]:
        sums = sums + ref[...]
    mean = sums[:, :1] / sums[:, 1:2]
    first, second = best_ref[:, :1], best_ref[:, 1:2]
    total = jnp.sum(total_ref[...], axis=1, keepdims=True)
    weighted = weighted_ref[...]
    largest = jnp.maximum(jnp.max(jnp.abs(weighted), axis=1, keepdims=True), 1e-30)
    coded = jnp.round(weighted * (STEPS / largest)).astype(jnp.int32).astype(jnp.int16)
    for h in range(SIDE):
        part = coded[h * step : (h + 1) * step].reshape(sources, pair, features)
        out_ref[:, :, h * features : (h + 1) * features] = part
    values = (
        parts(first, COSINE_UNIT)
        + parts(second, COSINE_UNIT)
        + parts(jnp.log(largest / total), LOG_UNIT)
        + parts(first - mean, NOVELTY_UNIT)
    )
    lane = lax.broadcasted_iota(jnp.int32, (step, EXTRA), 1)
    extra = jnp.zeros((step, EXTRA), jnp.float32)
    for k, value in enumerate(values):
        for h in range(SIDE):
            extra = jnp.where(lane == k + h * (EXTRA // SIDE), value[h * step : (h + 1) * step], extra)
    extra = extra.astype(jnp.int32).astype(jnp.int16)
    out_ref[:, :, SIDE * features :] = extra.reshape(sources, pair, EXTRA)


def joined(high, low, unit):
    return (high + low * (1.0 / LOW_UNIT)) * (1.0 / unit)


def pick_kernel(cluster_ref, back_ref, near_ref, best_ref, novelty_ref):
    across, down, i, j = cluster_pairs(cluster_ref)
    clusters, pair, width = back_ref.shape
    features = (width - EXTRA) // SIDE
    step = clusters * pair
    rank = jnp.sum(jnp.where((across == down) & (j < i), 1.0, 0.0), axis=1, keepdims=True)
    slot = slot_of(down[:, :1], rank.astype(jnp.int32), clusters)
    pick = jnp.where(lax.broadcasted_iota(jnp.int32, (i.shape[0], SIDE * step), 1) == slot, 1.0, 0.0)
    pick = pick.astype(jnp.bfloat16)

    pick = jnp.concatenate([pick, pick], axis=1)

    def mine(halves):
        value = jnp.concatenate(halves, axis=0).astype(jnp.float32)
        high = jnp.floor(value * (1.0 / 256.0)) * 256.0
        return dot(pick, jnp.concatenate([high, value - high], axis=0).astype(jnp.bfloat16), (1, 0))

    extra = back_ref[:, :, SIDE * features :].reshape(step, EXTRA).astype(jnp.float32)
    extra = mine([shifted(extra, h * (EXTRA // SIDE)) for h in range(SIDE)])
    largest = jnp.exp(joined(extra[:, 4:5], extra[:, 5:6], LOG_UNIT))
    rows = mine([back_ref[:, :, h * features : (h + 1) * features].reshape(step, features) for h in range(SIDE)])
    near_ref[...] = rows * (largest * (1.0 / STEPS))
    extra = extra.T
    best_ref[0:1, :] = joined(extra[0:1], extra[1:2], COSINE_UNIT)
    best_ref[1:2, :] = joined(extra[2:3], extra[3:4], COSINE_UNIT)
    novelty_ref[...] = joined(extra[6:7], extra[7:8], NOVELTY_UNIT)


def over_batch(value):
    n = lax.axis_size("batch")
    shifts = sorted(range(1, n), key=lambda k: -min(k, n - k))
    return [value] + [lax.ppermute(value, "batch", [(i, (i + k) % n) for i in range(n)]) for k in shifts]


def body(queries, query_cluster, store, store_counts):
    n_store = lax.axis_size("store")
    n_batch = lax.axis_size("batch")
    rows_dev, features = queries.shape
    clusters = store_counts.shape[0]
    crows = store.shape[0]
    depth = 2 * rows_dev // clusters
    slots = clusters * depth
    pair = depth // SIDE
    width = features + EXTRA
    wide = SIDE * features + EXTRA
    growth = math.log(3.0) / (rows_dev * n_store * n_batch)
    params = pltpu.CompilerParams(vmem_limit_bytes=VMEM_BYTES)

    cluster_row = query_cluster.reshape(1, rows_dev)
    send = pl.pallas_call(
        place_kernel,
        out_shape=jax.ShapeDtypeStruct((clusters, pair, wide), jnp.bfloat16),
        in_specs=[pl.BlockSpec(memory_space=pltpu.HBM)] * 2,
        scratch_shapes=[
            pltpu.VMEM((1, rows_dev), jnp.int32),
            pltpu.VMEM((rows_dev, features), jnp.bfloat16),
            pltpu.SemaphoreType.DMA,
            pltpu.SemaphoreType.DMA,
        ],
        compiler_params=pltpu.CompilerParams(vmem_limit_bytes=60 * 2**20),
    )(cluster_row, queries)

    info = jnp.stack([store_counts[lax.axis_index("store")], lax.axis_index("batch")])
    near = crows // 2
    f32, bf16 = jnp.float32, store.dtype
    vmem = pl.BlockSpec(memory_space=pltpu.VMEM)
    hbm = pl.BlockSpec(memory_space=pltpu.HBM)
    smem = pl.BlockSpec(memory_space=pltpu.SMEM)
    store_scale, store_near, store_rest = pl.pallas_call(
        scale_kernel,
        out_shape=(
            jax.ShapeDtypeStruct((1, crows), f32),
            jax.ShapeDtypeStruct((near, features), bf16),
            jax.ShapeDtypeStruct((crows - near, features), bf16),
        ),
        in_specs=[hbm],
        out_specs=(vmem,) * 3,
        scratch_shapes=[pltpu.SemaphoreType.DMA, pltpu.SemaphoreType.DMA],
        compiler_params=params,
        cost_estimate=pl.CostEstimate(flops=2 * crows * features, bytes_accessed=2 * crows * features, transcendentals=crows),
    )(store)
    got = lax.all_to_all(send, "store", split_axis=0, concat_axis=0, tiled=True)

    half_cost = pl.CostEstimate(flops=slots * crows * features, bytes_accessed=crows * features, transcendentals=0)
    cos_near, rows, state = pl.pallas_call(
        near_kernel,
        out_shape=(
            jax.ShapeDtypeStruct((slots, near), f32),
            jax.ShapeDtypeStruct((slots, width), bf16),
            jax.ShapeDtypeStruct((2, slots, 128), f32),
        ),
        in_specs=[smem, vmem, vmem, vmem],
        out_specs=(vmem,) * 3,
        compiler_params=params,
        cost_estimate=half_cost,
    )(info, got, store_near, store_scale)
    cos_rest, best, sums = pl.pallas_call(
        functools.partial(rest_kernel, growth, n_batch, rows_dev, n_store),
        out_shape=(
            jax.ShapeDtypeStruct((slots, crows - near), f32),
            jax.ShapeDtypeStruct((slots, 128), f32),
            jax.ShapeDtypeStruct((1, 128), f32),
        ),
        in_specs=[smem, vmem, vmem, vmem, vmem],
        out_specs=(vmem,) * 3,
        compiler_params=params,
        cost_estimate=half_cost,
    )(info, rows, state, store_rest, store_scale)
    sums = over_batch(sums)
    weighted, total = pl.pallas_call(
        weigh_kernel,
        out_shape=(
            jax.ShapeDtypeStruct((slots, features), jnp.float32),
            jax.ShapeDtypeStruct((slots, 128), jnp.float32),
        ),
        in_specs=[smem] + [vmem] * 5,
        out_specs=(vmem, vmem),
        scratch_shapes=[pltpu.VMEM((slots, crows), jnp.bfloat16)],
        compiler_params=params,
        cost_estimate=pl.CostEstimate(flops=4 * slots * crows * features, bytes_accessed=8 * crows * features, transcendentals=slots * crows),
    )(info, cos_near, cos_rest, best, store_near, store_rest)
    back = pl.pallas_call(
        code_kernel,
        out_shape=jax.ShapeDtypeStruct((n_store, pair, wide), jnp.int16),
        in_specs=[vmem] * (3 + n_batch),
        out_specs=vmem,
        compiler_params=params,
    )(weighted, total, best, *sums)
    back = lax.all_to_all(back, "store", split_axis=0, concat_axis=0, tiled=True)

    neighbours, best, novelty = pl.pallas_call(
        pick_kernel,
        out_shape=(
            jax.ShapeDtypeStruct((rows_dev, features), jnp.float32),
            jax.ShapeDtypeStruct((2, rows_dev), jnp.float32),
            jax.ShapeDtypeStruct((1, rows_dev), jnp.float32),
        ),
        compiler_params=params,
    )(cluster_row, back)
    return (best.T, novelty[0], neighbours)


def solution(mesh):
    in_specs = (P(("store", "batch"), None), P(("store", "batch")), P("store", None), P())
    out_specs = (P(("store", "batch"), None), P(("store", "batch")), P(("store", "batch"), None))
    return jax.shard_map(body, mesh=mesh, in_specs=in_specs, out_specs=out_specs, check_vma=False)
```
